256 devices in a mesh: ctx: 32 (over z, x_hi, core), head: 8 (over y, x_lo).
Axes of the slice: x: 4 (x_hi: 2, x_lo: 2; x = x_hi * 2 + x_lo), y: 4, z: 8, core: 2. Of those that a mesh axis runs over, the one named last changes fastest.
Arguments:
- target: bfloat16 [2048, 3072], P(('ctx', 'head')), may hold values from -6 to 6
- query_weight: bfloat16 [3072, 3072], P(None, 'head'), may hold values from -0.109375 to 0.109375
- source_keys: bfloat16 [65536, 3072], P('ctx', 'head'), may hold values from -210 to 210
- source_values: bfloat16 [65536, 3072], P('ctx', 'head'), may hold values from -6 to 6
- out_weight: bfloat16 [3072, 3072], P('head'), may hold values from -0.109375 to 0.109375
Outputs:
- attended: bfloat16 [2048, 3072], P(('ctx', 'head'))
The draws below stay inside these ranges and needn't reach their ends.
All inputs are finite; a program needn't handle non-finite values.
Results may differ from the reference program's by a relative error of at most 0.022.
Values may be sent and summed in bfloat16 or wider, within the bound.
No kernel may reach another device: no remote copies, remote signals or barrier semaphores. Data moves between devices by JAX's collectives and lax.ppermute only.
A program may use at most 64 MiB of HBM per device.

```python
import math
import jax
import jax.numpy as jnp
from jax import lax

D = 3072
HEADS = 24
HD = 128
TOKENS = 2048
SRC = 65536


def draw_source_keys(key, part):
    key = jax.random.fold_in(key, 7)
    first = jax.random.fold_in(key, 0)
    result = jnp.clip(3.0 * jax.random.normal(first, (SRC, HEADS * HD), jnp.float32), -18.0, 18.0)
    return result.astype(jnp.bfloat16)


def levels(key, dims, cuts, smallest, top_value):
    factor_of, own = 1.0, jax.random.fold_in(key, 6)
    for axis_at, parts in cuts:
        heights = jnp.exp(jax.random.uniform(jax.random.fold_in(own, axis_at), (parts,), jnp.float32, smallest / len(cuts), top_value / len(cuts)))
        factor_of = factor_of * jnp.repeat(heights, dims[axis_at] // parts).reshape([-1 if axis == axis_at else 1 for axis in range(len(dims))])
    return factor_of


def normal_values(key, dims, width, reach, cuts=(), dtype=jnp.bfloat16):
    gain = levels(key, dims, cuts, -0.22, 0.18) if cuts else 1.0
    array = jax.random.normal(key, dims, jnp.float32) * width * gain
    return jnp.minimum(jnp.maximum(array, -reach), reach).astype(dtype)


def setup_inputs(seed: int = 0) -> dict:
    splits = jax.random.split(jax.random.key(seed), 6)
    target = normal_values(splits[0], (TOKENS, D), 1.0, 6.0, ((0, 256),))
    query_weight = normal_values(splits[1], (D, HEADS * HD), D ** -0.5, 0.109375, ((1, 8),))
    source_keys = draw_source_keys(jax.random.fold_in(splits[5], 71), 0)
    source_values = normal_values(splits[3], (SRC, HEADS * HD), 1.0, 6.0, ((0, 32), (1, 8)))
    out_weight = normal_values(splits[4], (HEADS * HD, D), (HEADS * HD) ** -0.5, 0.109375, ((0, 8),))
    return {"target": target, "query_weight": query_weight, "source_keys": source_keys, "source_values": source_values, "out_weight": out_weight}


def one_head(head_queries, head_keys, head_values):
    key_block = head_keys.astype(jnp.float32)
    value_block = head_values.astype(jnp.float32)
    total_rows = head_queries.shape[0]
    block = min(512, total_rows)

    def attend_rows(rows_block):
        scores = jnp.dot(rows_block.astype(jnp.float32), key_block.T, precision=lax.Precision.HIGHEST)
        peak = lax.optimization_barrier(jnp.max(scores, axis=-1, keepdims=True))
        weights = jnp.exp(scores - peak)
        totals = lax.optimization_barrier(jnp.sum(weights, axis=-1))
        rounded = lax.optimization_barrier(weights.astype(jnp.bfloat16)).astype(jnp.float32)
        numerator = jnp.dot(rounded, value_block, precision=lax.Precision.HIGHEST)
        return numerator / totals[:, None]
    pieces = lax.map(attend_rows, head_queries.reshape(total_rows // block, block, -1))
    return pieces.reshape(total_rows, -1)

def reference(target, query_weight, source_keys, source_values, out_weight):
    scale = 1.0 / math.sqrt(HD)
    queries = (jnp.dot(target, query_weight, preferred_element_type=jnp.float32) * scale).astype(jnp.bfloat16)
    per_head_q = queries.reshape(TOKENS, HEADS, HD).transpose(1, 0, 2)
    per_head_k = source_keys.reshape(SRC, HEADS, HD).transpose(1, 0, 2)
    per_head_v = source_values.reshape(SRC, HEADS, HD).transpose(1, 0, 2)
    outputs = lax.map(lambda group: one_head(group[0], group[1], group[2]), (per_head_q, per_head_k, per_head_v))
    mixed = outputs.transpose(1, 0, 2).reshape(TOKENS, HEADS * HD).astype(jnp.bfloat16)
    return jnp.dot(mixed, out_weight, preferred_element_type=jnp.float32).astype(jnp.bfloat16)
```

```python
import functools
import math

import jax
import jax.numpy as jnp
from jax import lax
from jax.experimental import pallas as pl
from jax.experimental.pallas import tpu as pltpu
from jax.sharding import PartitionSpec as P

HD = 128
BLOCK = 512
GROUP = 1024
PART = 64
TAIL = 16
AHEAD = 2
MERGE_FLOPS = 10**10
LOG2E = math.log2(math.e)
Z = 8


def vmem():
    return pl.BlockSpec(memory_space=pltpu.VMEM)


def move(value, dz=0, dx=0, dcore=0):
    pairs = []
    for source in range(Z * 4):
        z, x, core = source // 4, source // 2 % 2, source % 2
        pairs.append((source, (z + dz) % Z * 4 + (x ^ dx) * 2 + (core ^ dcore)))
    return lax.ppermute(value, "ctx", pairs)


def carry(value, steps):
    pairs = []
    for source in range(Z * 4):
        z, core = source // 4, source % 2
        pairs.append((source, (z + (steps if core else -steps)) % Z * 4 + source % 4))
    return lax.ppermute(value, "ctx", pairs)


def exchange(value):
    return lax.all_to_all(value, "head", 0, 0)


def parts_of(level):
    high = level.astype(jnp.bfloat16).astype(jnp.float32)
    middle = (level - high).astype(jnp.bfloat16).astype(jnp.float32)
    return high, middle, level - high - middle


def project_kernel(rows, weight, out):
    result = jnp.dot(rows[...], weight[...], preferred_element_type=jnp.float32)
    out[...] = (result * (1.0 / math.sqrt(HD))).astype(jnp.bfloat16)


def repeat_kernel(value, out):
    for at in range(out.shape[0]):
        out[at] = value[...]


def attend_kernel(count, *refs):
    asked, (key_a, key_b, value_a, value_b), rest = refs[:count], refs[count : count + 4], refs[count + 4 :]
    outs, held, weights = rest[:count], rest[count : count + AHEAD + 1], rest[count + AHEAD + 1 :]
    heads = asked[0].shape[1] // HD
    half = key_a.shape[0]
    across = sum(ref.shape[0] for ref in asked)
    steps = [(head, at) for head in range(heads) for at in range(0, 2 * half, GROUP)]
    row = lax.broadcasted_iota(jnp.int32, (TAIL, across), 0)

    def columns(head):
        return slice(head * HD, (head + 1) * HD)

    def turned_queries(head):
        return jnp.transpose(jnp.concatenate([ref[:, columns(head)] for ref in asked], axis=0))

    queries = [turned_queries(head) for head in range(heads)]

    def score(step, part, peak):
        head, at = steps[step]
        keys, place = (key_a, at + part) if at < half else (key_b, at + part - half)
        block = LOG2E * jnp.dot(
            keys[place : place + BLOCK, columns(head)], queries[head], preferred_element_type=jnp.float32
        )
        held[step % len(held)][part : part + BLOCK, :] = block
        top = jnp.max(block.reshape(BLOCK // 8, 8, across), axis=0)
        return top if peak is None else jnp.maximum(peak, top)

    def weigh(step, start, peak, total):
        for part in range(start, start + BLOCK, PART):
            block = held[step % len(held)][part : part + PART, :].reshape(PART // 8, 8, across)
            block = jnp.exp2(block - peak[None])
            total = total + jnp.sum(block, axis=0)
            block = block.reshape(PART, across).astype(jnp.bfloat16)
            weights[step % 2][part : part + PART, :] = block
        return total

    def weighted(step):
        head, at = steps[step]
        values, place = (value_a, at) if at < half else (value_b, at - half)
        return jnp.dot(
            values[columns(head), place : place + GROUP],
            weights[step % 2][...],
            preferred_element_type=jnp.float32,
        )

    stats = jnp.zeros((TAIL, across), jnp.float32)
    numerator = None

    def add_values(step, rescale, top, total):
        nonlocal numerator, stats
        head, at = steps[step]
        here = weighted(step)
        numerator = here if at == 0 else numerator * rescale + here
        if at + GROUP == 2 * half:
            total = jnp.sum(total, axis=0, keepdims=True)
            partial = jnp.transpose(numerator / total).astype(jnp.bfloat16)
            place = 0
            for ref, out in zip(asked, outs):
                out[: ref.shape[0], columns(head)] = partial[place : place + ref.shape[0]]
                place += ref.shape[0]
            for index, part in enumerate(parts_of(top + LOG2E * jnp.log(total))):
                stats = jnp.where(row == head * 3 + index, part, stats)

    peaks = [None] * len(steps)

    def score_ahead(step, part):
        if step < len(steps):
            peaks[step] = score(step, part, peaks[step])

    for step in range(AHEAD):
        for part in range(0, GROUP, BLOCK):
            score_ahead(step, part)
    pending = top = total = None
    for step, (head, at) in enumerate(steps):
        rescale, highest = None, jnp.max(peaks[step], axis=0, keepdims=True)
        if at:
            highest = jnp.maximum(top, highest)
            rescale = jnp.exp2(top - highest)
            total = total * rescale
        else:
            total = jnp.zeros((8, across), jnp.float32)
        top = highest
        wide = jnp.broadcast_to(top, (8, across))
        for part in range(0, GROUP, BLOCK):
            score_ahead(step + AHEAD, part)
            total = weigh(step, part, wide, total)
            if part == 0 and pending:
                add_values(*pending)
        pending = (step, rescale, top, total)
    add_values(*pending)
    stats = stats.astype(jnp.bfloat16)
    place = 0
    for ref, out in zip(asked, outs):
        rows = ref.shape[0]
        out[rows:, :] = jnp.zeros((TAIL, heads * HD), jnp.bfloat16)
        out[rows:, :rows] = stats[:, place : place + rows]
        place += rows


def merged(parts, tails):
    rows = parts[0].shape[0]
    heads = parts[0].shape[1] // HD
    shares, levels = [], []
    for head in range(heads):
        heights = [sum(tail[3 * head + index : 3 * head + index + 1, :] for index in range(3)) for tail in tails]
        peak = heights[0]
        for height in heights[1:]:
            peak = jnp.maximum(peak, height)
        powers = [jnp.exp2(height - peak) for height in heights]
        total = sum(powers)
        shares += [power / total for power in powers]
        levels.append(peak + LOG2E * jnp.log(total))
    place = lax.broadcasted_iota(jnp.int32, (HD, rows), 0)
    table = jnp.zeros((HD, rows), jnp.float32)
    for index, share in enumerate(shares):
        table = jnp.where(place == index, share, table)
    table = jnp.transpose(table)
    means = []
    for head in range(heads):
        columns = slice(head * HD, (head + 1) * HD)
        mean = 0.0
        for index, part in enumerate(parts):
            at = head * len(parts) + index
            mean += table[:, at : at + 1] * part[:, columns].astype(jnp.float32)
        means.append(mean.astype(jnp.bfloat16))
    return jnp.concatenate(means, axis=1), levels


def tail_of(levels):
    width = levels[0].shape[1]
    row = lax.broadcasted_iota(jnp.int32, (TAIL, width), 0)
    tail = jnp.zeros((TAIL, width), jnp.float32)
    for head, level in enumerate(levels):
        for index, part in enumerate(parts_of(level)):
            tail = jnp.where(row == head * 3 + index, part, tail)
    return tail.astype(jnp.bfloat16)


def piece(ref, start, rows):
    tail = ref[ref.shape[0] - TAIL :, start : start + rows].astype(jnp.float32)
    return ref[start : start + rows, :], tail


def merge_kernel(starts, *refs):
    out = refs[-1]
    rows = out.shape[0] - TAIL
    mean, levels = merged(*zip(*[piece(ref, start, rows) for ref, start in zip(refs, starts)]))
    out[:rows, :] = mean
    out[rows:, :] = jnp.zeros((TAIL, out.shape[1]), jnp.bfloat16)
    out[rows:, :rows] = tail_of(levels)


def finish_kernel(*refs):
    weight, out = refs[-2:]
    rows = out.shape[0]
    mixed, _ = merged(*zip(*[piece(ref, 0, rows) for ref in refs[:-2]]))
    out[...] = jnp.dot(mixed, weight[...], preferred_element_type=jnp.float32).astype(jnp.bfloat16)


def call(kernel, name, out_shape, operands, flops=0, read=0, exps=0, limit=16, scratch=()):
    return pl.pallas_call(
        kernel,
        out_shape=out_shape,
        in_specs=[vmem()] * len(operands),
        out_specs=jax.tree.map(lambda _: vmem(), out_shape),
        scratch_shapes=scratch,
        compiler_params=pltpu.CompilerParams(vmem_limit_bytes=limit << 20),
        cost_estimate=pl.CostEstimate(flops=flops, bytes_accessed=read, transcendentals=exps),
        name=name,
    )(*operands)


def shape(*dims):
    return jax.ShapeDtypeStruct(dims, jnp.bfloat16)


def project(rows, weight):
    out_shape = shape(rows.shape[0], weight.shape[1])
    flops = 2 * rows.shape[0] * weight.size
    return call(project_kernel, "project", out_shape, (rows, weight), flops, 2 * weight.size)


def repeat(value, count):
    return call(repeat_kernel, "repeat", shape(count, *value.shape), (value,), MERGE_FLOPS)


def attend(asked, keys, values):
    width = asked[0].shape[1]
    across = sum(queries.shape[0] for queries in asked)
    pairs = 2 * across * keys[0].shape[0] * (width // HD)
    out_shape = [shape(queries.shape[0] + TAIL, width) for queries in asked]
    scratch = [pltpu.VMEM((GROUP, across), kind) for kind in (jnp.float32,) * (AHEAD + 1) + (jnp.bfloat16,) * 2]
    kernel = functools.partial(attend_kernel, len(asked))
    operands = (*asked, *keys, *values)
    return call(kernel, "attend", out_shape, operands, 8 * pairs * HD, 8 * keys[0].size, pairs, 32, scratch)


def turn_kernel(value, out):
    for head in range(value.shape[1] // HD):
        out[head * HD : (head + 1) * HD, :] = jnp.transpose(value[:, head * HD : (head + 1) * HD])


def turn(value):
    return call(turn_kernel, "turn", shape(*value.shape[::-1]), (value,), 0, 4 * value.size)


def merge(rows, *places):
    parts, starts = zip(*places)
    out_shape = shape(rows + TAIL, parts[0].shape[1])
    return call(functools.partial(merge_kernel, starts), "merge", out_shape, parts, MERGE_FLOPS)


def finish(parts, weight):
    out_shape = shape(parts[-1].shape[0] - TAIL, weight.shape[1])
    flops = 2 * out_shape.shape[0] * weight.size
    return call(finish_kernel, "finish", out_shape, (*parts, weight), flops, 2 * weight.size)


def tied(*values):
    return lax.optimization_barrier(values)


def shards(target, query_weight, source_keys, source_values, out_weight):
    groups = lax.axis_size("head")
    rows, depth = target.shape
    keys = (source_keys, move(source_keys, dcore=1))
    other_values = move(source_values, dcore=1)
    gathered = exchange(repeat(target, groups))
    queries = project(gathered.reshape(groups * rows, depth), query_weight)
    few = queries.shape[0]
    queries, source_values = tied(queries, source_values)
    partner, turned = tied(move(queries, dx=1), turn(source_values))
    mine = jnp.concatenate([queries, partner], axis=0)
    sibling, other_values = tied(move(mine, dcore=1), other_values)
    near = carry(jnp.concatenate([mine, sibling], axis=0), 1)
    values = (turned, turn(other_values))
    part_own, = attend((mine,), keys, values)
    part_own, near = tied(part_own, near)
    second = carry(near, 1)
    part, = attend((near,), keys, values)
    part, second = tied(part, second)
    third, far = carry(second, 1), carry(second[: 2 * few], 2)
    back_near = carry(part, -1)
    part, = attend((third,), keys, values)
    part, second, far, back_near = tied(part, second, far, back_near)
    back_third = carry(part, -3)
    part_far, = attend((far,), keys, values)
    part_far, second = tied(part_far, second)
    back_far = carry(part_far, -4)
    part, = attend((second,), keys, values)
    early = merge(2 * few, (part_own, 0), (back_far, 0), (back_near, 0), (back_third, 0))
    back_second, early = tied(carry(part, -2), early)
    others = merge(2 * few, *[(part, 2 * few) for part in (back_near, back_second, back_third)])
    others = move(others, dcore=1)
    kept = merge(2 * few, (early, 0), (back_second, 0))
    other = move(merge(few, (kept, few), (others, few)), dx=1)
    projected = finish((kept, others, other), out_weight)
    received = exchange(projected.reshape(groups, rows, depth))
    return jnp.sum(received.astype(jnp.float32), axis=0).astype(jnp.bfloat16)


def solution(mesh):
    in_specs = (
        P(("ctx", "head"), None),
        P(None, "head"),
        P("ctx", "head"),
        P("ctx", "head"),
        P("head", None),
    )
    out_specs = P(("ctx", "head"), None)
    return jax.shard_map(shards, mesh=mesh, in_specs=in_specs, out_specs=out_specs, check_vma=False)
```

```python
import functools
import math

import jax
import jax.numpy as jnp
from jax import lax
from jax.experimental import pallas as pl
from jax.experimental.pallas import tpu as pltpu
from jax.sharding import PartitionSpec as P

HD = 128
BLOCK = 512
GROUP = 1024
PART = 64
TAIL = 16
AHEAD = 2
MERGE_FLOPS = 10**10
LOG2E = math.log2(math.e)
Z = 8


def vmem():
    return pl.BlockSpec(memory_space=pltpu.VMEM)


def move(value, dz=0, dx=0, dcore=0):
    pairs = []
    for source in range(Z * 4):
        z, x, core = source // 4, source // 2 % 2, source % 2
        pairs.append((source, (z + dz) % Z * 4 + (x ^ dx) * 2 + (core ^ dcore)))
    return lax.ppermute(value, "ctx", pairs)


def carry(value, steps):
    pairs = []
    for source in range(Z * 4):
        z, core = source // 4, source % 2
        pairs.append((source, (z + (steps if core else -steps)) % Z * 4 + source % 4))
    return lax.ppermute(value, "ctx", pairs)


def exchange(value):
    return lax.all_to_all(value, "head", 0, 0)


def parts_of(level):
    high = level.astype(jnp.bfloat16).astype(jnp.float32)
    middle = (level - high).astype(jnp.bfloat16).astype(jnp.float32)
    return high, middle, level - high - middle


def project_kernel(rows, weight, out):
    result = jnp.dot(rows[...], weight[...], preferred_element_type=jnp.float32)
    out[...] = (result * (1.0 / math.sqrt(HD))).astype(jnp.bfloat16)


def repeat_kernel(value, out):
    for at in range(out.shape[0]):
        out[at] = value[...]


def attend_kernel(count, *refs):
    asked, (key_a, key_b, value_a, value_b), rest = refs[:count], refs[count : count + 4], refs[count + 4 :]
    outs, held, weights = rest[:count], rest[count : count + AHEAD + 1], rest[count + AHEAD + 1 :]
    heads = asked[0].shape[1] // HD
    half = key_a.shape[0]
    across = sum(ref.shape[0] for ref in asked)
    steps = [(head, at) for head in range(heads) for at in range(0, 2 * half, GROUP)]
    row = lax.broadcasted_iota(jnp.int32, (TAIL, across), 0)

    def columns(head):
        return slice(head * HD, (head + 1) * HD)

    def turned_queries(head):
        return jnp.transpose(jnp.concatenate([ref[:, columns(head)] for ref in asked], axis=0))

    queries = [turned_queries(head) for head in range(heads)]

    def score(step, part, peak):
        head, at = steps[step]
        keys, place = (key_a, at + part) if at < half else (key_b, at + part - half)
        block = LOG2E * jnp.dot(
            keys[place : place + BLOCK, columns(head)], queries[head], preferred_element_type=jnp.float32
        )
        held[step % len(held)][part : part + BLOCK, :] = block
        top = jnp.max(block.reshape(BLOCK // 8, 8, across), axis=0)
        return top if peak is None else jnp.maximum(peak, top)

    def weigh(step, start, peak, total):
        for part in range(start, start + BLOCK, PART):
            block = held[step % len(held)][part : part + PART, :].reshape(PART // 8, 8, across)
            block = jnp.exp2(block - peak[None])
            total = total + jnp.sum(block, axis=0)
            block = block.reshape(PART, across).astype(jnp.bfloat16)
            weights[step % 2][part : part + PART, :] = block
        return total

    def weighted(step):
        head, at = steps[step]
        values, place = (value_a, at) if at < half else (value_b, at - half)
        return jnp.dot(
            values[columns(head), place : place + GROUP],
            weights[step % 2][...],
            preferred_element_type=jnp.float32,
        )

    stats = jnp.zeros((TAIL, across), jnp.float32)
    numerator = None

    def add_values(step, rescale, top, total):
        nonlocal numerator, stats
        head, at = steps[step]
        here = weighted(step)
        numerator = here if at == 0 else numerator * rescale + here
        if at + GROUP == 2 * half:
            total = jnp.sum(total, axis=0, keepdims=True)
            partial = jnp.transpose(numerator / total).astype(jnp.bfloat16)
            place = 0
            for ref, out in zip(asked, outs):
                out[: ref.shape[0], columns(head)] = partial[place : place + ref.shape[0]]
                place += ref.shape[0]
            for index, part in enumerate(parts_of(top + LOG2E * jnp.log(total))):
                stats = jnp.where(row == head * 3 + index, part, stats)

    peaks = [None] * len(steps)

    def score_ahead(step, part):
        if step < len(steps):
            peaks[step] = score(step, part, peaks[step])

    for step in range(AHEAD):
        for part in range(0, GROUP, BLOCK):
            score_ahead(step, part)
    pending = top = total = None
    for step, (head, at) in enumerate(steps):
        rescale, highest = None, jnp.max(peaks[step], axis=0, keepdims=True)
        if at:
            highest = jnp.maximum(top, highest)
            rescale = jnp.exp2(top - highest)
            total = total * rescale
        else:
            total = jnp.zeros((8, across), jnp.float32)
        top = highest
        wide = jnp.broadcast_to(top, (8, across))
        for part in range(0, GROUP, BLOCK):
            total = weigh(step, part, wide, total)
            score_ahead(step + AHEAD, part)
            if part == 0 and pending:
                add_values(*pending)
        pending = (step, rescale, top, total)
    add_values(*pending)
    stats = stats.astype(jnp.bfloat16)
    place = 0
    for ref, out in zip(asked, outs):
        rows = ref.shape[0]
        out[rows:, :] = jnp.zeros((TAIL, heads * HD), jnp.bfloat16)
        out[rows:, :rows] = stats[:, place : place + rows]
        place += rows


def merged(parts, tails):
    rows = parts[0].shape[0]
    heads = parts[0].shape[1] // HD
    shares, levels = [], []
    for head in range(heads):
        heights = [sum(tail[3 * head + index : 3 * head + index + 1, :] for index in range(3)) for tail in tails]
        peak = heights[0]
        for height in heights[1:]:
            peak = jnp.maximum(peak, height)
        powers = [jnp.exp2(height - peak) for height in heights]
        total = sum(powers)
        shares += [power / total for power in powers]
        levels.append(peak + LOG2E * jnp.log(total))
    place = lax.broadcasted_iota(jnp.int32, (HD, rows), 0)
    table = jnp.zeros((HD, rows), jnp.float32)
    for index, share in enumerate(shares):
        table = jnp.where(place == index, share, table)
    table = jnp.transpose(table)
    means = []
    for head in range(heads):
        columns = slice(head * HD, (head + 1) * HD)
        mean = 0.0
        for index, part in enumerate(parts):
            at = head * len(parts) + index
            mean += table[:, at : at + 1] * part[:, columns].astype(jnp.float32)
        means.append(mean.astype(jnp.bfloat16))
    return jnp.concatenate(means, axis=1), levels


def tail_of(levels):
    width = levels[0].shape[1]
    row = lax.broadcasted_iota(jnp.int32, (TAIL, width), 0)
    tail = jnp.zeros((TAIL, width), jnp.float32)
    for head, level in enumerate(levels):
        for index, part in enumerate(parts_of(level)):
            tail = jnp.where(row == head * 3 + index, part, tail)
    return tail.astype(jnp.bfloat16)


def piece(ref, start, rows):
    tail = ref[ref.shape[0] - TAIL :, start : start + rows].astype(jnp.float32)
    return ref[start : start + rows, :], tail


def merge_kernel(starts, *refs):
    out = refs[-1]
    rows = out.shape[0] - TAIL
    mean, levels = merged(*zip(*[piece(ref, start, rows) for ref, start in zip(refs, starts)]))
    out[:rows, :] = mean
    out[rows:, :] = jnp.zeros((TAIL, out.shape[1]), jnp.bfloat16)
    out[rows:, :rows] = tail_of(levels)


def finish_kernel(*refs):
    weight, out = refs[-2:]
    rows = out.shape[0]
    mixed, _ = merged(*zip(*[piece(ref, 0, rows) for ref in refs[:-2]]))
    out[...] = jnp.dot(mixed, weight[...], preferred_element_type=jnp.float32).astype(jnp.bfloat16)


def call(kernel, name, out_shape, operands, flops=0, read=0, exps=0, limit=16, scratch=()):
    return pl.pallas_call(
        kernel,
        out_shape=out_shape,
        in_specs=[vmem()] * len(operands),
        out_specs=jax.tree.map(lambda _: vmem(), out_shape),
        scratch_shapes=scratch,
        compiler_params=pltpu.CompilerParams(vmem_limit_bytes=limit << 20),
        cost_estimate=pl.CostEstimate(flops=flops, bytes_accessed=read, transcendentals=exps),
        name=name,
    )(*operands)


def shape(*dims):
    return jax.ShapeDtypeStruct(dims, jnp.bfloat16)


def project(rows, weight):
    out_shape = shape(rows.shape[0], weight.shape[1])
    flops = 2 * rows.shape[0] * weight.size
    return call(project_kernel, "project", out_shape, (rows, weight), flops, 2 * weight.size)


def repeat(value, count):
    return call(repeat_kernel, "repeat", shape(count, *value.shape), (value,), MERGE_FLOPS)


def attend(asked, keys, values):
    width = asked[0].shape[1]
    across = sum(queries.shape[0] for queries in asked)
    pairs = 2 * across * keys[0].shape[0] * (width // HD)
    out_shape = [shape(queries.shape[0] + TAIL, width) for queries in asked]
    scratch = [pltpu.VMEM((GROUP, across), kind) for kind in (jnp.float32,) * (AHEAD + 1) + (jnp.bfloat16,) * 2]
    kernel = functools.partial(attend_kernel, len(asked))
    operands = (*asked, *keys, *values)
    return call(kernel, "attend", out_shape, operands, 8 * pairs * HD, 8 * keys[0].size, pairs, 32, scratch)


def turn_kernel(value, out):
    for head in range(value.shape[1] // HD):
        out[head * HD : (head + 1) * HD, :] = jnp.transpose(value[:, head * HD : (head + 1) * HD])


def turn(value):
    return call(turn_kernel, "turn", shape(*value.shape[::-1]), (value,), 0, 4 * value.size)


def merge(rows, *places, flops=0):
    parts, starts = zip(*places)
    out_shape = shape(rows + TAIL, parts[0].shape[1])
    return call(functools.partial(merge_kernel, starts), "merge", out_shape, parts, flops)


def finish(parts, weight):
    out_shape = shape(parts[-1].shape[0] - TAIL, weight.shape[1])
    flops = 2 * out_shape.shape[0] * weight.size
    return call(finish_kernel, "finish", out_shape, (*parts, weight), flops, 2 * weight.size)


def tied(*values):
    return lax.optimization_barrier(values)


def shards(target, query_weight, source_keys, source_values, out_weight):
    groups = lax.axis_size("head")
    rows, depth = target.shape
    keys = (source_keys, move(source_keys, dcore=1))
    other_values = move(source_values, dcore=1)
    gathered = exchange(repeat(target, groups))
    queries = project(gathered.reshape(groups * rows, depth), query_weight)
    few = queries.shape[0]
    queries, source_values = tied(queries, source_values)
    partner, turned = tied(move(queries, dx=1), turn(source_values))
    mine = jnp.concatenate([queries, partner], axis=0)
    sibling, other_values = tied(move(mine, dcore=1), other_values)
    near = carry(jnp.concatenate([mine, sibling], axis=0), 1)
    values = (turned, turn(other_values))
    part_own, = attend((mine,), keys, values)
    part_own, near = tied(part_own, near)
    second = carry(near, 1)
    part, = attend((near,), keys, values)
    part, second = tied(part, second)
    third, far = carry(second, 1), carry(second[: 2 * few], 2)
    back_near = carry(part, -1)
    part_others, = attend((second[2 * few :],), keys, values)
    part_others, third, back_near = tied(part_others, third, back_near)
    back_others = carry(part_others, -2)
    part, = attend((third,), keys, values)
    part, second, far = tied(part, second, far)
    back_third = carry(part, -3)
    part_far, = attend((far,), keys, values)
    part_far, second, back_others = tied(part_far, second, back_others)
    back_far = carry(part_far, -4)
    part, = attend((second[: 2 * few],), keys, values)
    early = merge(2 * few, (part_own, 0), (back_far, 0), (back_near, 0), (back_third, 0), flops=MERGE_FLOPS)
    others = move(merge(2 * few, (back_others, 0), (back_near, 2 * few), (back_third, 2 * few)), dcore=1)
    back_second, early, others = tied(carry(part, -2), early, others)
    kept = merge(2 * few, (early, 0), (back_second, 0))
    other = move(merge(few, (kept, few), (others, few)), dx=1)
    projected = finish((kept, others, other), out_weight)
    received = exchange(projected.reshape(groups, rows, depth))
    return jnp.sum(received.astype(jnp.float32), axis=0).astype(jnp.bfloat16)


def solution(mesh):
    in_specs = (
        P(("ctx", "head"), None),
        P(None, "head"),
        P("ctx", "head"),
        P("ctx", "head"),
        P("head", None),
    )
    out_specs = P(("ctx", "head"), None)
    return jax.shard_map(shards, mesh=mesh, in_specs=in_specs, out_specs=out_specs, check_vma=False)
```

```python
import functools
import math

import jax
import jax.numpy as jnp
from jax import lax
from jax.experimental import pallas as pl
from jax.experimental.pallas import tpu as pltpu
from jax.sharding import PartitionSpec as P

HD = 128
BLOCK = 512
GROUP = 1024
PART = 64
TAIL = 16
AHEAD = 2
MERGE_FLOPS = 10**10
LOG2E = math.log2(math.e)
Z = 8


def vmem():
    return pl.BlockSpec(memory_space=pltpu.VMEM)


def move(value, dz=0, dx=0, dcore=0):
    pairs = []
    for source in range(Z * 4):
        z, x, core = source // 4, source // 2 % 2, source % 2
        pairs.append((source, (z + dz) % Z * 4 + (x ^ dx) * 2 + (core ^ dcore)))
    return lax.ppermute(value, "ctx", pairs)


def carry(value, steps):
    pairs = []
    for source in range(Z * 4):
        z, core = source // 4, source % 2
        pairs.append((source, (z + (steps if core else -steps)) % Z * 4 + source % 4))
    return lax.ppermute(value, "ctx", pairs)


def exchange(value):
    return lax.all_to_all(value, "head", 0, 0)


def parts_of(level):
    high = level.astype(jnp.bfloat16).astype(jnp.float32)
    middle = (level - high).astype(jnp.bfloat16).astype(jnp.float32)
    return high, middle, level - high - middle


def project_kernel(rows, weight, out):
    result = jnp.dot(rows[...], weight[...], preferred_element_type=jnp.float32)
    out[...] = (result * (1.0 / math.sqrt(HD))).astype(jnp.bfloat16)


def repeat_kernel(value, out):
    for at in range(out.shape[0]):
        out[at] = value[...]


def attend_kernel(count, *refs):
    asked, (key_a, key_b, value_a, value_b), rest = refs[:count], refs[count : count + 4], refs[count + 4 :]
    outs, held, weights = rest[:count], rest[count : count + AHEAD + 1], rest[count + AHEAD + 1 :]
    heads = asked[0].shape[1] // HD
    half = key_a.shape[0]
    across = sum(ref.shape[0] for ref in asked)
    steps = [(head, at) for head in range(heads) for at in range(0, 2 * half, GROUP)]
    row = lax.broadcasted_iota(jnp.int32, (TAIL, across), 0)

    def columns(head):
        return slice(head * HD, (head + 1) * HD)

    def turned_queries(head):
        return jnp.transpose(jnp.concatenate([ref[:, columns(head)] for ref in asked], axis=0))

    queries = [turned_queries(head) for head in range(heads)]

    def score(step, part, peak):
        head, at = steps[step]
        keys, place = (key_a, at + part) if at < half else (key_b, at + part - half)
        block = LOG2E * jnp.dot(
            keys[place : place + BLOCK, columns(head)], queries[head], preferred_element_type=jnp.float32
        )
        held[step % len(held)][part : part + BLOCK, :] = block
        top = jnp.max(block.reshape(BLOCK // 8, 8, across), axis=0)
        return top if peak is None else jnp.maximum(peak, top)

    def weigh(step, start, peak, total):
        for part in range(start, start + BLOCK, PART):
            block = held[step % len(held)][part : part + PART, :].reshape(PART // 8, 8, across)
            block = jnp.exp2(block - peak[None])
            total = total + jnp.sum(block, axis=0)
            block = block.reshape(PART, across).astype(jnp.bfloat16)
            weights[step % 2][part : part + PART, :] = block
        return total

    def weighted(step):
        head, at = steps[step]
        values, place = (value_a, at) if at < half else (value_b, at - half)
        return jnp.dot(
            values[columns(head), place : place + GROUP],
            weights[step % 2][...],
            preferred_element_type=jnp.float32,
        )

    stats = jnp.zeros((TAIL, across), jnp.float32)
    numerator = None

    def add_values(step, rescale, top, total):
        nonlocal numerator, stats
        head, at = steps[step]
        here = weighted(step)
        numerator = here if at == 0 else numerator * rescale + here
        if at + GROUP == 2 * half:
            total = jnp.sum(total, axis=0, keepdims=True)
            partial = jnp.transpose(numerator / total).astype(jnp.bfloat16)
            place = 0
            for ref, out in zip(asked, outs):
                out[: ref.shape[0], columns(head)] = partial[place : place + ref.shape[0]]
                place += ref.shape[0]
            for index, part in enumerate(parts_of(top + LOG2E * jnp.log(total))):
                stats = jnp.where(row == head * 3 + index, part, stats)

    peaks = [None] * len(steps)

    def score_ahead(step, part):
        if step < len(steps):
            peaks[step] = score(step, part, peaks[step])

    for step in range(AHEAD):
        for part in range(0, GROUP, BLOCK):
            score_ahead(step, part)
    pending = top = total = None
    for step, (head, at) in enumerate(steps):
        rescale, highest = None, jnp.max(peaks[step], axis=0, keepdims=True)
        if at:
            highest = jnp.maximum(top, highest)
            rescale = jnp.exp2(top - highest)
            total = total * rescale
        else:
            total = jnp.zeros((8, across), jnp.float32)
        top = highest
        wide = jnp.broadcast_to(top, (8, across))
        for part in range(0, GROUP, BLOCK):
            score_ahead(step + AHEAD, part)
            total = weigh(step, part, wide, total)
            if part == 0 and pending:
                add_values(*pending)
        pending = (step, rescale, top, total)
    add_values(*pending)
    stats = stats.astype(jnp.bfloat16)
    place = 0
    for ref, out in zip(asked, outs):
        rows = ref.shape[0]
        out[rows:, :] = jnp.zeros((TAIL, heads * HD), jnp.bfloat16)
        out[rows:, :rows] = stats[:, place : place + rows]
        place += rows


def merged(parts, tails):
    rows = parts[0].shape[0]
    heads = parts[0].shape[1] // HD
    shares, levels = [], []
    for head in range(heads):
        heights = [sum(tail[3 * head + index : 3 * head + index + 1, :] for index in range(3)) for tail in tails]
        peak = heights[0]
        for height in heights[1:]:
            peak = jnp.maximum(peak, height)
        powers = [jnp.exp2(height - peak) for height in heights]
        total = sum(powers)
        shares += [power / total for power in powers]
        levels.append(peak + LOG2E * jnp.log(total))
    place = lax.broadcasted_iota(jnp.int32, (HD, rows), 0)
    table = jnp.zeros((HD, rows), jnp.float32)
    for index, share in enumerate(shares):
        table = jnp.where(place == index, share, table)
    table = jnp.transpose(table)
    means = []
    for head in range(heads):
        columns = slice(head * HD, (head + 1) * HD)
        mean = 0.0
        for index, part in enumerate(parts):
            at = head * len(parts) + index
            mean += table[:, at : at + 1] * part[:, columns].astype(jnp.float32)
        means.append(mean.astype(jnp.bfloat16))
    return jnp.concatenate(means, axis=1), levels


def tail_of(levels):
    width = levels[0].shape[1]
    row = lax.broadcasted_iota(jnp.int32, (TAIL, width), 0)
    tail = jnp.zeros((TAIL, width), jnp.float32)
    for head, level in enumerate(levels):
        for index, part in enumerate(parts_of(level)):
            tail = jnp.where(row == head * 3 + index, part, tail)
    return tail.astype(jnp.bfloat16)


def piece(ref, start, rows):
    tail = ref[ref.shape[0] - TAIL :, start : start + rows].astype(jnp.float32)
    return ref[start : start + rows, :], tail


def merge_kernel(starts, *refs):
    out = refs[-1]
    rows = out.shape[0] - TAIL
    mean, levels = merged(*zip(*[piece(ref, start, rows) for ref, start in zip(refs, starts)]))
    out[:rows, :] = mean
    out[rows:, :] = jnp.zeros((TAIL, out.shape[1]), jnp.bfloat16)
    out[rows:, :rows] = tail_of(levels)


def finish_kernel(*refs):
    weight, out = refs[-2:]
    rows = out.shape[0]
    mixed, _ = merged(*zip(*[piece(ref, 0, rows) for ref in refs[:-2]]))
    out[...] = jnp.dot(mixed, weight[...], preferred_element_type=jnp.float32).astype(jnp.bfloat16)


def call(kernel, name, out_shape, operands, flops=0, read=0, exps=0, limit=16, scratch=()):
    return pl.pallas_call(
        kernel,
        out_shape=out_shape,
        in_specs=[vmem()] * len(operands),
        out_specs=jax.tree.map(lambda _: vmem(), out_shape),
        scratch_shapes=scratch,
        compiler_params=pltpu.CompilerParams(vmem_limit_bytes=limit << 20),
        cost_estimate=pl.CostEstimate(flops=flops, bytes_accessed=read, transcendentals=exps),
        name=name,
    )(*operands)


def shape(*dims):
    return jax.ShapeDtypeStruct(dims, jnp.bfloat16)


def project(rows, weight):
    out_shape = shape(rows.shape[0], weight.shape[1])
    flops = 2 * rows.shape[0] * weight.size
    return call(project_kernel, "project", out_shape, (rows, weight), flops, 2 * weight.size)


def repeat(value, count):
    return call(repeat_kernel, "repeat", shape(count, *value.shape), (value,), MERGE_FLOPS)


def attend(asked, keys, values):
    width = asked[0].shape[1]
    across = sum(queries.shape[0] for queries in asked)
    pairs = 2 * across * keys[0].shape[0] * (width // HD)
    out_shape = [shape(queries.shape[0] + TAIL, width) for queries in asked]
    scratch = [pltpu.VMEM((GROUP, across), kind) for kind in (jnp.float32,) * (AHEAD + 1) + (jnp.bfloat16,) * 2]
    kernel = functools.partial(attend_kernel, len(asked))
    operands = (*asked, *keys, *values)
    return call(kernel, "attend", out_shape, operands, 8 * pairs * HD, 8 * keys[0].size, pairs, 32, scratch)


def turn_kernel(value, out):
    for head in range(value.shape[1] // HD):
        out[head * HD : (head + 1) * HD, :] = jnp.transpose(value[:, head * HD : (head + 1) * HD])


def turn(value):
    return call(turn_kernel, "turn", shape(*value.shape[::-1]), (value,), 0, 4 * value.size)


def merge(rows, *places, flops=0):
    parts, starts = zip(*places)
    out_shape = shape(rows + TAIL, parts[0].shape[1])
    return call(functools.partial(merge_kernel, starts), "merge", out_shape, parts, flops)


def finish(parts, weight):
    out_shape = shape(parts[-1].shape[0] - TAIL, weight.shape[1])
    flops = 2 * out_shape.shape[0] * weight.size
    return call(finish_kernel, "finish", out_shape, (*parts, weight), flops, 2 * weight.size)


def tied(*values):
    return lax.optimization_barrier(values)


def shards(target, query_weight, source_keys, source_values, out_weight):
    groups = lax.axis_size("head")
    rows, depth = target.shape
    keys = (source_keys, move(source_keys, dcore=1))
    other_values = move(source_values, dcore=1)
    gathered = exchange(repeat(target, groups))
    queries = project(gathered.reshape(groups * rows, depth), query_weight)
    few = queries.shape[0]
    queries, source_values = tied(queries, source_values)
    partner, turned = tied(move(queries, dx=1), turn(source_values))
    mine = jnp.concatenate([queries, partner], axis=0)
    sibling, other_values = tied(move(mine, dcore=1), other_values)
    near = carry(jnp.concatenate([mine, sibling], axis=0), 1)
    values = (turned, turn(other_values))
    part_own, = attend((mine,), keys, values)
    part_own, near = tied(part_own, near)
    second = carry(near, 1)
    part, = attend((near,), keys, values)
    part, second = tied(part, second)
    third, far = carry(second, 1), carry(second[: 2 * few], 2)
    back_near = carry(part, -1)
    part_others, = attend((second[2 * few :],), keys, values)
    part_others, third, back_near = tied(part_others, third, back_near)
    back_others = carry(part_others, -2)
    part, = attend((third,), keys, values)
    part, second, far = tied(part, second, far)
    back_third = carry(part, -3)
    part_far, = attend((far,), keys, values)
    part_far, second = tied(part_far, second)
    back_far = carry(part_far, -4)
    part, = attend((second[: 2 * few],), keys, values)
    early = merge(2 * few, (part_own, 0), (back_far, 0), (back_near, 0), (back_third, 0), flops=MERGE_FLOPS)
    others = move(merge(2 * few, (back_others, 0), (back_near, 2 * few), (back_third, 2 * few)), dcore=1)
    back_second, early, others = tied(carry(part, -2), early, others)
    kept = merge(2 * few, (early, 0), (back_second, 0))
    other = move(merge(few, (kept, few), (others, few)), dx=1)
    projected = finish((kept, others, other), out_weight)
    received = exchange(projected.reshape(groups, rows, depth))
    return jnp.sum(received.astype(jnp.float32), axis=0).astype(jnp.bfloat16)


def solution(mesh):
    in_specs = (
        P(("ctx", "head"), None),
        P(None, "head"),
        P("ctx", "head"),
        P("ctx", "head"),
        P("head", None),
    )
    out_specs = P(("ctx", "head"), None)
    return jax.shard_map(shards, mesh=mesh, in_specs=in_specs, out_specs=out_specs, check_vma=False)
```

```python
import functools
import math

import jax
import jax.numpy as jnp
from jax import lax
from jax.experimental import pallas as pl
from jax.experimental.pallas import tpu as pltpu
from jax.sharding import PartitionSpec as P

HD = 128
BLOCK = 512
GROUP = 1024
PART = 64
TAIL = 16
AHEAD = 2
MERGE_FLOPS = 10**10
LOG2E = math.log2(math.e)
Z = 8


def vmem():
    return pl.BlockSpec(memory_space=pltpu.VMEM)


def move(value, dz=0, dx=0, dcore=0):
    pairs = []
    for source in range(Z * 4):
        z, x, core = source // 4, source // 2 % 2, source % 2
        pairs.append((source, (z + dz) % Z * 4 + (x ^ dx) * 2 + (core ^ dcore)))
    return lax.ppermute(value, "ctx", pairs)


def carry(value, steps):
    pairs = []
    for source in range(Z * 4):
        z, core = source // 4, source % 2
        pairs.append((source, (z + (steps if core else -steps)) % Z * 4 + source % 4))
    return lax.ppermute(value, "ctx", pairs)


def exchange(value):
    return lax.all_to_all(value, "head", 0, 0)


def parts_of(level):
    high = level.astype(jnp.bfloat16).astype(jnp.float32)
    middle = (level - high).astype(jnp.bfloat16).astype(jnp.float32)
    return high, middle, level - high - middle


def project_kernel(rows, weight, out):
    result = jnp.dot(rows[...], weight[...], preferred_element_type=jnp.float32)
    out[...] = (result * (1.0 / math.sqrt(HD))).astype(jnp.bfloat16)


def repeat_kernel(value, out):
    for at in range(out.shape[0]):
        out[at] = value[...]


def attend_kernel(count, *refs):
    asked, (key_a, key_b, value_a, value_b), rest = refs[:count], refs[count : count + 4], refs[count + 4 :]
    outs, turned, rest = rest[:count], rest[count], rest[count + 1 :]
    heads = asked[0].shape[1] // HD
    half = key_a.shape[0]
    groups = 2 * half // GROUP
    held, weights = rest[:groups], rest[groups:]
    across = sum(ref.shape[0] for ref in asked)
    row = lax.broadcasted_iota(jnp.int32, (TAIL, across), 0)

    def columns(head):
        return pl.ds(pl.multiple_of(head * HD, HD), HD)

    def score(head, group, part, peak):
        at = group * GROUP + part
        keys, place = (key_a, at) if at < half else (key_b, at - half)
        block = LOG2E * jnp.dot(
            keys[place : place + BLOCK, columns(head)], turned[head], preferred_element_type=jnp.float32
        )
        held[group][part : part + BLOCK, :] = block
        top = jnp.max(block.reshape(BLOCK // 8, 8, across), axis=0)
        return top if peak is None else jnp.maximum(peak, top)

    def weigh(group, start, peak, total):
        for part in range(start, start + BLOCK, PART):
            block = held[group][part : part + PART, :].reshape(PART // 8, 8, across)
            block = jnp.exp2(block - peak[None])
            total = total + jnp.sum(block, axis=0)
            block = block.reshape(PART, across).astype(jnp.bfloat16)
            weights[group % 2][part : part + PART, :] = block
        return total

    def weighted(head, group):
        at = group * GROUP
        values, place = (value_a, at) if at < half else (value_b, at - half)
        return jnp.dot(
            values[columns(head), place : place + GROUP], weights[group % 2][...], preferred_element_type=jnp.float32
        )

    for head in range(heads):
        block = jnp.concatenate([ref[:, head * HD : (head + 1) * HD] for ref in asked], axis=0)
        turned[head] = jnp.transpose(block)

    def one_head(head, carry):
        *peaks, stats = carry
        peaks = peaks + [None] * groups
        after = jnp.minimum(head + 1, heads - 1)
        top = total = numerator = pending = None

        def add_values(numerator, group, rescale):
            here = weighted(head, group)
            return here if numerator is None else numerator * rescale + here

        for group in range(groups):
            rescale, highest = None, jnp.max(peaks[group], axis=0, keepdims=True)
            if group:
                highest = jnp.maximum(top, highest)
                rescale = jnp.exp2(top - highest)
                total = total * rescale
            else:
                total = jnp.zeros((8, across), jnp.float32)
            top = highest
            wide = jnp.broadcast_to(top, (8, across))
            then = group + AHEAD
            for part in range(0, GROUP, BLOCK):
                peaks[then] = score(head if then < groups else after, then % groups, part, peaks[then])
                total = weigh(group, part, wide, total)
                if part == 0 and pending:
                    numerator = add_values(numerator, *pending)
            pending = (group, rescale)
        numerator = add_values(numerator, *pending)
        total = jnp.sum(total, axis=0, keepdims=True)
        partial = jnp.transpose(numerator / total).astype(jnp.bfloat16)
        place = 0
        for ref, out in zip(asked, outs):
            out[: ref.shape[0], columns(head)] = partial[place : place + ref.shape[0]]
            place += ref.shape[0]
        for index, part in enumerate(parts_of(top + LOG2E * jnp.log(total))):
            stats = jnp.where(row == head * 3 + index, part, stats)
        return (*peaks[groups:], stats)

    first = [None] * AHEAD
    for group in range(AHEAD):
        for part in range(0, GROUP, BLOCK):
            first[group] = score(0, group, part, first[group])
    *_, stats = lax.fori_loop(0, heads, one_head, (*first, jnp.zeros((TAIL, across), jnp.float32)))
    stats = stats.astype(jnp.bfloat16)
    place = 0
    for ref, out in zip(asked, outs):
        rows = ref.shape[0]
        out[rows:, :] = jnp.zeros((TAIL, heads * HD), jnp.bfloat16)
        out[rows:, :rows] = stats[:, place : place + rows]
        place += rows


def merged(parts, tails):
    rows = parts[0].shape[0]
    heads = parts[0].shape[1] // HD
    shares, levels = [], []
    for head in range(heads):
        heights = [sum(tail[3 * head + index : 3 * head + index + 1, :] for index in range(3)) for tail in tails]
        peak = heights[0]
        for height in heights[1:]:
            peak = jnp.maximum(peak, height)
        powers = [jnp.exp2(height - peak) for height in heights]
        total = sum(powers)
        shares += [power / total for power in powers]
        levels.append(peak + LOG2E * jnp.log(total))
    place = lax.broadcasted_iota(jnp.int32, (HD, rows), 0)
    table = jnp.zeros((HD, rows), jnp.float32)
    for index, share in enumerate(shares):
        table = jnp.where(place == index, share, table)
    table = jnp.transpose(table)
    means = []
    for head in range(heads):
        columns = slice(head * HD, (head + 1) * HD)
        mean = 0.0
        for index, part in enumerate(parts):
            at = head * len(parts) + index
            mean += table[:, at : at + 1] * part[:, columns].astype(jnp.float32)
        means.append(mean.astype(jnp.bfloat16))
    return jnp.concatenate(means, axis=1), levels


def tail_of(levels):
    width = levels[0].shape[1]
    row = lax.broadcasted_iota(jnp.int32, (TAIL, width), 0)
    tail = jnp.zeros((TAIL, width), jnp.float32)
    for head, level in enumerate(levels):
        for index, part in enumerate(parts_of(level)):
            tail = jnp.where(row == head * 3 + index, part, tail)
    return tail.astype(jnp.bfloat16)


def piece(ref, start, rows):
    tail = ref[ref.shape[0] - TAIL :, start : start + rows].astype(jnp.float32)
    return ref[start : start + rows, :], tail


def merge_kernel(starts, *refs):
    out = refs[-1]
    rows = out.shape[0] - TAIL
    mean, levels = merged(*zip(*[piece(ref, start, rows) for ref, start in zip(refs, starts)]))
    out[:rows, :] = mean
    out[rows:, :] = jnp.zeros((TAIL, out.shape[1]), jnp.bfloat16)
    out[rows:, :rows] = tail_of(levels)


def finish_kernel(*refs):
    weight, out = refs[-2:]
    rows = out.shape[0]
    mixed, _ = merged(*zip(*[piece(ref, 0, rows) for ref in refs[:-2]]))
    out[...] = jnp.dot(mixed, weight[...], preferred_element_type=jnp.float32).astype(jnp.bfloat16)


def call(kernel, name, out_shape, operands, flops=0, read=0, exps=0, limit=16, scratch=()):
    return pl.pallas_call(
        kernel,
        out_shape=out_shape,
        in_specs=[vmem()] * len(operands),
        out_specs=jax.tree.map(lambda _: vmem(), out_shape),
        scratch_shapes=scratch,
        compiler_params=pltpu.CompilerParams(vmem_limit_bytes=limit << 20),
        cost_estimate=pl.CostEstimate(flops=flops, bytes_accessed=read, transcendentals=exps),
        name=name,
    )(*operands)


def shape(*dims):
    return jax.ShapeDtypeStruct(dims, jnp.bfloat16)


def project(rows, weight):
    out_shape = shape(rows.shape[0], weight.shape[1])
    flops = 2 * rows.shape[0] * weight.size
    return call(project_kernel, "project", out_shape, (rows, weight), flops, 2 * weight.size)


def repeat(value, count):
    return call(repeat_kernel, "repeat", shape(count, *value.shape), (value,), MERGE_FLOPS)


def attend(asked, keys, values):
    width = asked[0].shape[1]
    across = sum(queries.shape[0] for queries in asked)
    pairs = 2 * across * keys[0].shape[0] * (width // HD)
    out_shape = [shape(queries.shape[0] + TAIL, width) for queries in asked]
    groups = 2 * keys[0].shape[0] // GROUP
    scratch = [pltpu.VMEM((width // HD, HD, across), jnp.bfloat16)]
    scratch += [pltpu.VMEM((GROUP, across), kind) for kind in (jnp.float32,) * groups + (jnp.bfloat16,) * 2]
    kernel = functools.partial(attend_kernel, len(asked))
    operands = (*asked, *keys, *values)
    return call(kernel, "attend", out_shape, operands, 8 * pairs * HD, 8 * keys[0].size, pairs, 32, scratch)


def turn_kernel(value, out):
    for head in range(value.shape[1] // HD):
        out[head * HD : (head + 1) * HD, :] = jnp.transpose(value[:, head * HD : (head + 1) * HD])


def turn(value):
    return call(turn_kernel, "turn", shape(*value.shape[::-1]), (value,), 0, 4 * value.size)


def merge(rows, *places, flops=0):
    parts, starts = zip(*places)
    out_shape = shape(rows + TAIL, parts[0].shape[1])
    return call(functools.partial(merge_kernel, starts), "merge", out_shape, parts, flops)


def finish(parts, weight):
    out_shape = shape(parts[-1].shape[0] - TAIL, weight.shape[1])
    flops = 2 * out_shape.shape[0] * weight.size
    return call(finish_kernel, "finish", out_shape, (*parts, weight), flops, 2 * weight.size)


def tied(*values):
    return lax.optimization_barrier(values)


def shards(target, query_weight, source_keys, source_values, out_weight):
    groups = lax.axis_size("head")
    rows, depth = target.shape
    keys = (source_keys, move(source_keys, dcore=1))
    other_values = move(source_values, dcore=1)
    gathered = exchange(repeat(target, groups))
    queries = project(gathered.reshape(groups * rows, depth), query_weight)
    few = queries.shape[0]
    queries, source_values = tied(queries, source_values)
    partner, turned = tied(move(queries, dx=1), turn(source_values))
    mine = jnp.concatenate([queries, partner], axis=0)
    sibling, other_values = tied(move(mine, dcore=1), other_values)
    near = carry(jnp.concatenate([mine, sibling], axis=0), 1)
    values = (turned, turn(other_values))
    part_own, = attend((mine,), keys, values)
    part_own, near = tied(part_own, near)
    second = carry(near, 1)
    part, = attend((near,), keys, values)
    part, second = tied(part, second)
    third, far = carry(second, 1), carry(second[: 2 * few], 2)
    back_near = carry(part, -1)
    part_others, = attend((second[2 * few :],), keys, values)
    part_others, third, back_near = tied(part_others, third, back_near)
    back_others = carry(part_others, -2)
    part, = attend((third,), keys, values)
    part, second, far = tied(part, second, far)
    back_third = carry(part, -3)
    part_far, = attend((far,), keys, values)
    part_far, second = tied(part_far, second)
    back_far = carry(part_far, -4)
    part, = attend((second[: 2 * few],), keys, values)
    early = merge(2 * few, (part_own, 0), (back_far, 0), (back_near, 0), (back_third, 0), flops=MERGE_FLOPS)
    others = move(merge(2 * few, (back_others, 0), (back_near, 2 * few), (back_third, 2 * few)), dcore=1)
    back_second, early, others = tied(carry(part, -2), early, others)
    kept = merge(2 * few, (early, 0), (back_second, 0))
    other = move(merge(few, (kept, few), (others, few)), dx=1)
    projected = finish((kept, others, other), out_weight)
    received = exchange(projected.reshape(groups, rows, depth))
    return jnp.sum(received.astype(jnp.float32), axis=0).astype(jnp.bfloat16)


def solution(mesh):
    in_specs = (
        P(("ctx", "head"), None),
        P(None, "head"),
        P("ctx", "head"),
        P("ctx", "head"),
        P("head", None),
    )
    out_specs = P(("ctx", "head"), None)
    return jax.shard_map(shards, mesh=mesh, in_specs=in_specs, out_specs=out_specs, check_vma=False)
```

```python
import functools
import math

import jax
import jax.numpy as jnp
from jax import lax
from jax.experimental import pallas as pl
from jax.experimental.pallas import tpu as pltpu
from jax.sharding import PartitionSpec as P

HD = 128
BLOCK = 512
GROUP = 1024
PART = 64
TAIL = 16
AHEAD = 2
MERGE_FLOPS = 10**10
LOG2E = math.log2(math.e)
Z = 8


def vmem():
    return pl.BlockSpec(memory_space=pltpu.VMEM)


def move(value, dz=0, dx=0, dcore=0):
    pairs = []
    for source in range(Z * 4):
        z, x, core = source // 4, source // 2 % 2, source % 2
        pairs.append((source, (z + dz) % Z * 4 + (x ^ dx) * 2 + (core ^ dcore)))
    return lax.ppermute(value, "ctx", pairs)


def carry(value, steps):
    pairs = []
    for source in range(Z * 4):
        z, core = source // 4, source % 2
        pairs.append((source, (z + (-steps if core else steps)) % Z * 4 + source % 4))
    return lax.ppermute(value, "ctx", pairs)


def exchange(value):
    return lax.all_to_all(value, "head", 0, 0)


def parts_of(level):
    high = level.astype(jnp.bfloat16).astype(jnp.float32)
    middle = (level - high).astype(jnp.bfloat16).astype(jnp.float32)
    return high, middle, level - high - middle


def project_kernel(rows, weight, out):
    result = jnp.dot(rows[...], weight[...], preferred_element_type=jnp.float32)
    out[...] = (result * (1.0 / math.sqrt(HD))).astype(jnp.bfloat16)


def repeat_kernel(value, out):
    for at in range(out.shape[0]):
        out[at] = value[...]


def attend_kernel(count, *refs):
    asked, (key_a, key_b, value_a, value_b), rest = refs[:count], refs[count : count + 4], refs[count + 4 :]
    outs, held, weights = rest[:count], rest[count : count + AHEAD + 1], rest[count + AHEAD + 1 :]
    heads = asked[0].shape[1] // HD
    half = key_a.shape[0]
    across = sum(ref.shape[0] for ref in asked)
    steps = [(head, at) for head in range(heads) for at in range(0, 2 * half, GROUP)]
    row = lax.broadcasted_iota(jnp.int32, (TAIL, across), 0)

    def columns(head):
        return slice(head * HD, (head + 1) * HD)

    def turned_queries(head):
        return jnp.transpose(jnp.concatenate([ref[:, columns(head)] for ref in asked], axis=0))

    queries = [turned_queries(head) for head in range(heads)]

    def score(step, part, peak):
        head, at = steps[step]
        keys, place = (key_a, at + part) if at < half else (key_b, at + part - half)
        block = LOG2E * jnp.dot(
            keys[place : place + BLOCK, columns(head)], queries[head], preferred_element_type=jnp.float32
        )
        held[step % len(held)][part : part + BLOCK, :] = block
        top = jnp.max(block.reshape(BLOCK // 8, 8, across), axis=0)
        return top if peak is None else jnp.maximum(peak, top)

    def weigh(step, start, peak, total):
        for part in range(start, start + BLOCK, PART):
            block = held[step % len(held)][part : part + PART, :].reshape(PART // 8, 8, across)
            block = jnp.exp2(block - peak[None])
            total = total + jnp.sum(block, axis=0)
            block = block.reshape(PART, across).astype(jnp.bfloat16)
            weights[step % 2][part : part + PART, :] = block
        return total

    def weighted(step):
        head, at = steps[step]
        values, place = (value_a, at) if at < half else (value_b, at - half)
        return jnp.dot(
            values[columns(head), place : place + GROUP],
            weights[step % 2][...],
            preferred_element_type=jnp.float32,
        )

    stats = jnp.zeros((TAIL, across), jnp.float32)
    numerator = None

    def add_values(step, rescale, top, total):
        nonlocal numerator, stats
        head, at = steps[step]
        here = weighted(step)
        numerator = here if at == 0 else numerator * rescale + here
        if at + GROUP == 2 * half:
            total = jnp.sum(total, axis=0, keepdims=True)
            partial = jnp.transpose(numerator / total).astype(jnp.bfloat16)
            place = 0
            for ref, out in zip(asked, outs):
                out[: ref.shape[0], columns(head)] = partial[place : place + ref.shape[0]]
                place += ref.shape[0]
            for index, part in enumerate(parts_of(top + LOG2E * jnp.log(total))):
                stats = jnp.where(row == head * 3 + index, part, stats)

    peaks = [None] * len(steps)

    def score_ahead(step, part):
        if step < len(steps):
            peaks[step] = score(step, part, peaks[step])

    for step in range(AHEAD):
        for part in range(0, GROUP, BLOCK):
            score_ahead(step, part)
    pending = top = total = None
    for step, (head, at) in enumerate(steps):
        rescale, highest = None, jnp.max(peaks[step], axis=0, keepdims=True)
        if at:
            highest = jnp.maximum(top, highest)
            rescale = jnp.exp2(top - highest)
            total = total * rescale
        else:
            total = jnp.zeros((8, across), jnp.float32)
        top = highest
        wide = jnp.broadcast_to(top, (8, across))
        for part in range(0, GROUP, BLOCK):
            score_ahead(step + AHEAD, part)
            total = weigh(step, part, wide, total)
            if part == 0 and pending:
                add_values(*pending)
        pending = (step, rescale, top, total)
    add_values(*pending)
    stats = stats.astype(jnp.bfloat16)
    place = 0
    for ref, out in zip(asked, outs):
        rows = ref.shape[0]
        out[rows:, :] = jnp.zeros((TAIL, heads * HD), jnp.bfloat16)
        out[rows:, :rows] = stats[:, place : place + rows]
        place += rows


def merged(parts, tails):
    rows = parts[0].shape[0]
    heads = parts[0].shape[1] // HD
    shares, levels = [], []
    for head in range(heads):
        heights = [sum(tail[3 * head + index : 3 * head + index + 1, :] for index in range(3)) for tail in tails]
        peak = heights[0]
        for height in heights[1:]:
            peak = jnp.maximum(peak, height)
        powers = [jnp.exp2(height - peak) for height in heights]
        total = sum(powers)
        shares += [power / total for power in powers]
        levels.append(peak + LOG2E * jnp.log(total))
    place = lax.broadcasted_iota(jnp.int32, (HD, rows), 0)
    table = jnp.zeros((HD, rows), jnp.float32)
    for index, share in enumerate(shares):
        table = jnp.where(place == index, share, table)
    table = jnp.transpose(table)
    means = []
    for head in range(heads):
        columns = slice(head * HD, (head + 1) * HD)
        mean = 0.0
        for index, part in enumerate(parts):
            at = head * len(parts) + index
            mean += table[:, at : at + 1] * part[:, columns].astype(jnp.float32)
        means.append(mean.astype(jnp.bfloat16))
    return jnp.concatenate(means, axis=1), levels


def tail_of(levels):
    width = levels[0].shape[1]
    row = lax.broadcasted_iota(jnp.int32, (TAIL, width), 0)
    tail = jnp.zeros((TAIL, width), jnp.float32)
    for head, level in enumerate(levels):
        for index, part in enumerate(parts_of(level)):
            tail = jnp.where(row == head * 3 + index, part, tail)
    return tail.astype(jnp.bfloat16)


def piece(ref, start, rows):
    tail = ref[ref.shape[0] - TAIL :, start : start + rows].astype(jnp.float32)
    return ref[start : start + rows, :], tail


def merge_kernel(starts, *refs):
    out = refs[-1]
    rows = out.shape[0] - TAIL
    mean, levels = merged(*zip(*[piece(ref, start, rows) for ref, start in zip(refs, starts)]))
    out[:rows, :] = mean
    out[rows:, :] = jnp.zeros((TAIL, out.shape[1]), jnp.bfloat16)
    out[rows:, :rows] = tail_of(levels)


def finish_kernel(*refs):
    weight, out = refs[-2:]
    rows = out.shape[0]
    mixed, _ = merged(*zip(*[piece(ref, 0, rows) for ref in refs[:-2]]))
    out[...] = jnp.dot(mixed, weight[...], preferred_element_type=jnp.float32).astype(jnp.bfloat16)


def call(kernel, name, out_shape, operands, flops=0, read=0, exps=0, limit=16, scratch=()):
    return pl.pallas_call(
        kernel,
        out_shape=out_shape,
        in_specs=[vmem()] * len(operands),
        out_specs=jax.tree.map(lambda _: vmem(), out_shape),
        scratch_shapes=scratch,
        compiler_params=pltpu.CompilerParams(vmem_limit_bytes=limit << 20),
        cost_estimate=pl.CostEstimate(flops=flops, bytes_accessed=read, transcendentals=exps),
        name=name,
    )(*operands)


def shape(*dims):
    return jax.ShapeDtypeStruct(dims, jnp.bfloat16)


def project(rows, weight):
    out_shape = shape(rows.shape[0], weight.shape[1])
    flops = 2 * rows.shape[0] * weight.size
    return call(project_kernel, "project", out_shape, (rows, weight), flops, 2 * weight.size)


def repeat(value, count):
    return call(repeat_kernel, "repeat", shape(count, *value.shape), (value,), MERGE_FLOPS)


def attend(asked, keys, values):
    width = asked[0].shape[1]
    across = sum(queries.shape[0] for queries in asked)
    pairs = 2 * across * keys[0].shape[0] * (width // HD)
    out_shape = [shape(queries.shape[0] + TAIL, width) for queries in asked]
    scratch = [pltpu.VMEM((GROUP, across), kind) for kind in (jnp.float32,) * (AHEAD + 1) + (jnp.bfloat16,) * 2]
    kernel = functools.partial(attend_kernel, len(asked))
    operands = (*asked, *keys, *values)
    return call(kernel, "attend", out_shape, operands, 8 * pairs * HD, 8 * keys[0].size, pairs, 32, scratch)


def turn_kernel(value, out):
    for head in range(value.shape[1] // HD):
        out[head * HD : (head + 1) * HD, :] = jnp.transpose(value[:, head * HD : (head + 1) * HD])


def turn(value):
    return call(turn_kernel, "turn", shape(*value.shape[::-1]), (value,), 0, 4 * value.size)


def merge(rows, *places, flops=0):
    parts, starts = zip(*places)
    out_shape = shape(rows + TAIL, parts[0].shape[1])
    return call(functools.partial(merge_kernel, starts), "merge", out_shape, parts, flops)


def finish(parts, weight):
    out_shape = shape(parts[-1].shape[0] - TAIL, weight.shape[1])
    flops = 2 * out_shape.shape[0] * weight.size
    return call(finish_kernel, "finish", out_shape, (*parts, weight), flops, 2 * weight.size)


def tied(*values):
    return lax.optimization_barrier(values)


def shards(target, query_weight, source_keys, source_values, out_weight):
    groups = lax.axis_size("head")
    rows, depth = target.shape
    keys = (source_keys, move(source_keys, dcore=1))
    other_values = move(source_values, dcore=1)
    gathered = exchange(repeat(target, groups))
    queries = project(gathered.reshape(groups * rows, depth), query_weight)
    few = queries.shape[0]
    queries, source_values = tied(queries, source_values)
    partner, turned = tied(move(queries, dx=1), turn(source_values))
    mine = jnp.concatenate([queries, partner], axis=0)
    sibling, other_values = tied(move(mine, dcore=1), other_values)
    near = carry(jnp.concatenate([mine, sibling], axis=0), 1)
    values = (turned, turn(other_values))
    part_own, = attend((mine,), keys, values)
    part_own, near = tied(part_own, near)
    second = carry(near, 1)
    part, = attend((near,), keys, values)
    part, second = tied(part, second)
    third, far = carry(second, 1), carry(second[: 2 * few], 2)
    back_near = carry(part, -1)
    part_others, = attend((second[2 * few :],), keys, values)
    part_others, third, back_near = tied(part_others, third, back_near)
    back_others = carry(part_others, -2)
    part, = attend((third,), keys, values)
    part, second, far, back_others = tied(part, second, far, back_others)
    back_third = carry(part, -3)
    part_far, = attend((far,), keys, values)
    part_far, second = tied(part_far, second)
    back_far = carry(part_far, -4)
    part, = attend((second[: 2 * few],), keys, values)
    early = merge(2 * few, (part_own, 0), (back_far, 0), (back_near, 0), (back_third, 0), flops=MERGE_FLOPS)
    others = move(merge(2 * few, (back_others, 0), (back_near, 2 * few), (back_third, 2 * few)), dcore=1)
    back_second, early, others = tied(carry(part, -2), early, others)
    kept = merge(2 * few, (early, 0), (back_second, 0))
    other = move(merge(few, (kept, few), (others, few)), dx=1)
    projected = finish((kept, others, other), out_weight)
    received = exchange(projected.reshape(groups, rows, depth))
    return jnp.sum(received.astype(jnp.float32), axis=0).astype(jnp.bfloat16)


def solution(mesh):
    in_specs = (
        P(("ctx", "head"), None),
        P(None, "head"),
        P("ctx", "head"),
        P("ctx", "head"),
        P("head", None),
    )
    out_specs = P(("ctx", "head"), None)
    return jax.shard_map(shards, mesh=mesh, in_specs=in_specs, out_specs=out_specs, check_vma=False)
```

```python
import functools
import math

import jax
import jax.numpy as jnp
from jax import lax
from jax.experimental import pallas as pl
from jax.experimental.pallas import tpu as pltpu
from jax.sharding import PartitionSpec as P

HD = 128
BLOCK = 512
GROUP = 1024
PART = 64
TAIL = 16
AHEAD = 2
MERGE_FLOPS = 10**10
LOG2E = math.log2(math.e)
Z = 8


def vmem():
    return pl.BlockSpec(memory_space=pltpu.VMEM)


def move(value, dz=0, dx=0, dcore=0):
    pairs = []
    for source in range(Z * 4):
        z, x, core = source // 4, source // 2 % 2, source % 2
        pairs.append((source, (z + dz) % Z * 4 + (x ^ dx) * 2 + (core ^ dcore)))
    return lax.ppermute(value, "ctx", pairs)


def carry(value, steps):
    pairs = []
    for source in range(Z * 4):
        z, core = source // 4, source % 2
        pairs.append((source, (z + (-steps if core else steps)) % Z * 4 + source % 4))
    return lax.ppermute(value, "ctx", pairs)


def exchange(value):
    return lax.all_to_all(value, "head", 0, 0)


def parts_of(level):
    high = level.astype(jnp.bfloat16).astype(jnp.float32)
    middle = (level - high).astype(jnp.bfloat16).astype(jnp.float32)
    return high, middle, level - high - middle


def project_kernel(rows, weight, out):
    result = jnp.dot(rows[...], weight[...], preferred_element_type=jnp.float32)
    out[...] = (result * (1.0 / math.sqrt(HD))).astype(jnp.bfloat16)


def repeat_kernel(value, out):
    for at in range(out.shape[0]):
        out[at] = value[...]


def attend_kernel(count, *refs):
    asked, (key_a, key_b, value_a, value_b), rest = refs[:count], refs[count : count + 4], refs[count + 4 :]
    outs, held, weights = rest[:count], rest[count : count + AHEAD + 1], rest[count + AHEAD + 1 :]
    heads = asked[0].shape[1] // HD
    half = key_a.shape[0]
    across = sum(ref.shape[0] for ref in asked)
    steps = [(head, at) for head in range(heads) for at in range(0, 2 * half, GROUP)]
    row = lax.broadcasted_iota(jnp.int32, (TAIL, across), 0)

    def columns(head):
        return slice(head * HD, (head + 1) * HD)

    def turned_queries(head):
        return jnp.transpose(jnp.concatenate([ref[:, columns(head)] for ref in asked], axis=0))

    queries = [turned_queries(head) for head in range(heads)]

    def score(step, part, peak):
        head, at = steps[step]
        keys, place = (key_a, at + part) if at < half else (key_b, at + part - half)
        block = jnp.dot(
            keys[place : place + BLOCK, columns(head)], queries[head], preferred_element_type=jnp.float32
        )
        held[step % len(held)][part : part + BLOCK, :] = block
        top = jnp.max(block.reshape(BLOCK // 8, 8, across), axis=0)
        return top if peak is None else jnp.maximum(peak, top)

    def weigh(step, start, peak, total):
        for part in range(start, start + BLOCK, PART):
            block = held[step % len(held)][part : part + PART, :].reshape(PART // 8, 8, across)
            block = jnp.exp2(LOG2E * block - peak[None])
            total = total + jnp.sum(block, axis=0)
            block = block.reshape(PART, across).astype(jnp.bfloat16)
            weights[step % 2][part : part + PART, :] = block
        return total

    def weighted(step):
        head, at = steps[step]
        values, place = (value_a, at) if at < half else (value_b, at - half)
        return jnp.dot(
            values[columns(head), place : place + GROUP],
            weights[step % 2][...],
            preferred_element_type=jnp.float32,
        )

    stats = jnp.zeros((TAIL, across), jnp.float32)
    numerator = None

    def add_values(step, rescale, top, total):
        nonlocal numerator, stats
        head, at = steps[step]
        here = weighted(step)
        numerator = here if at == 0 else numerator * rescale + here
        if at + GROUP == 2 * half:
            total = jnp.sum(total, axis=0, keepdims=True)
            partial = jnp.transpose(numerator / total).astype(jnp.bfloat16)
            place = 0
            for ref, out in zip(asked, outs):
                out[: ref.shape[0], columns(head)] = partial[place : place + ref.shape[0]]
                place += ref.shape[0]
            for index, part in enumerate(parts_of(top + LOG2E * jnp.log(total))):
                stats = jnp.where(row == head * 3 + index, part, stats)

    peaks = [None] * len(steps)

    def score_ahead(step, part):
        if step < len(steps):
            peaks[step] = score(step, part, peaks[step])

    for step in range(AHEAD):
        for part in range(0, GROUP, BLOCK):
            score_ahead(step, part)
    pending = top = total = None
    for step, (head, at) in enumerate(steps):
        rescale, highest = None, LOG2E * jnp.max(peaks[step], axis=0, keepdims=True)
        if at:
            highest = jnp.maximum(top, highest)
            rescale = jnp.exp2(top - highest)
            total = total * rescale
        else:
            total = jnp.zeros((8, across), jnp.float32)
        top = highest
        wide = jnp.broadcast_to(top, (8, across))
        for part in range(0, GROUP, BLOCK):
            score_ahead(step + AHEAD, part)
            total = weigh(step, part, wide, total)
            if part == 0 and pending:
                add_values(*pending)
        pending = (step, rescale, top, total)
    add_values(*pending)
    stats = stats.astype(jnp.bfloat16)
    place = 0
    for ref, out in zip(asked, outs):
        rows = ref.shape[0]
        out[rows:, :] = jnp.zeros((TAIL, heads * HD), jnp.bfloat16)
        out[rows:, :rows] = stats[:, place : place + rows]
        place += rows


def merged(parts, tails):
    rows = parts[0].shape[0]
    heads = parts[0].shape[1] // HD
    shares, levels = [], []
    for head in range(heads):
        heights = [sum(tail[3 * head + index : 3 * head + index + 1, :] for index in range(3)) for tail in tails]
        peak = heights[0]
        for height in heights[1:]:
            peak = jnp.maximum(peak, height)
        powers = [jnp.exp2(height - peak) for height in heights]
        total = sum(powers)
        shares += [power / total for power in powers]
        levels.append(peak + LOG2E * jnp.log(total))
    place = lax.broadcasted_iota(jnp.int32, (HD, rows), 0)
    table = jnp.zeros((HD, rows), jnp.float32)
    for index, share in enumerate(shares):
        table = jnp.where(place == index, share, table)
    table = jnp.transpose(table)
    means = []
    for head in range(heads):
        columns = slice(head * HD, (head + 1) * HD)
        mean = 0.0
        for index, part in enumerate(parts):
            at = head * len(parts) + index
            mean += table[:, at : at + 1] * part[:, columns].astype(jnp.float32)
        means.append(mean.astype(jnp.bfloat16))
    return jnp.concatenate(means, axis=1), levels


def tail_of(levels):
    width = levels[0].shape[1]
    row = lax.broadcasted_iota(jnp.int32, (TAIL, width), 0)
    tail = jnp.zeros((TAIL, width), jnp.float32)
    for head, level in enumerate(levels):
        for index, part in enumerate(parts_of(level)):
            tail = jnp.where(row == head * 3 + index, part, tail)
    return tail.astype(jnp.bfloat16)


def piece(ref, start, rows):
    tail = ref[ref.shape[0] - TAIL :, start : start + rows].astype(jnp.float32)
    return ref[start : start + rows, :], tail


def merge_kernel(starts, *refs):
    out = refs[-1]
    rows = out.shape[0] - TAIL
    mean, levels = merged(*zip(*[piece(ref, start, rows) for ref, start in zip(refs, starts)]))
    out[:rows, :] = mean
    out[rows:, :] = jnp.zeros((TAIL, out.shape[1]), jnp.bfloat16)
    out[rows:, :rows] = tail_of(levels)


def finish_kernel(*refs):
    weight, out = refs[-2:]
    rows = out.shape[0]
    mixed, _ = merged(*zip(*[piece(ref, 0, rows) for ref in refs[:-2]]))
    out[...] = jnp.dot(mixed, weight[...], preferred_element_type=jnp.float32).astype(jnp.bfloat16)


def call(kernel, name, out_shape, operands, flops=0, read=0, exps=0, limit=16, scratch=()):
    return pl.pallas_call(
        kernel,
        out_shape=out_shape,
        in_specs=[vmem()] * len(operands),
        out_specs=jax.tree.map(lambda _: vmem(), out_shape),
        scratch_shapes=scratch,
        compiler_params=pltpu.CompilerParams(vmem_limit_bytes=limit << 20),
        cost_estimate=pl.CostEstimate(flops=flops, bytes_accessed=read, transcendentals=exps),
        name=name,
    )(*operands)


def shape(*dims):
    return jax.ShapeDtypeStruct(dims, jnp.bfloat16)


def project(rows, weight):
    out_shape = shape(rows.shape[0], weight.shape[1])
    flops = 2 * rows.shape[0] * weight.size
    return call(project_kernel, "project", out_shape, (rows, weight), flops, 2 * weight.size)


def repeat(value, count):
    return call(repeat_kernel, "repeat", shape(count, *value.shape), (value,), MERGE_FLOPS)


def attend(asked, keys, values):
    width = asked[0].shape[1]
    across = sum(queries.shape[0] for queries in asked)
    pairs = 2 * across * keys[0].shape[0] * (width // HD)
    out_shape = [shape(queries.shape[0] + TAIL, width) for queries in asked]
    scratch = [pltpu.VMEM((GROUP, across), kind) for kind in (jnp.float32,) * (AHEAD + 1) + (jnp.bfloat16,) * 2]
    kernel = functools.partial(attend_kernel, len(asked))
    operands = (*asked, *keys, *values)
    return call(kernel, "attend", out_shape, operands, 8 * pairs * HD, 8 * keys[0].size, pairs, 32, scratch)


def turn_kernel(value, out):
    for head in range(value.shape[1] // HD):
        out[head * HD : (head + 1) * HD, :] = jnp.transpose(value[:, head * HD : (head + 1) * HD])


def turn(value):
    return call(turn_kernel, "turn", shape(*value.shape[::-1]), (value,), 0, 4 * value.size)


def merge(rows, *places, flops=0):
    parts, starts = zip(*places)
    out_shape = shape(rows + TAIL, parts[0].shape[1])
    return call(functools.partial(merge_kernel, starts), "merge", out_shape, parts, flops)


def finish(parts, weight):
    out_shape = shape(parts[-1].shape[0] - TAIL, weight.shape[1])
    flops = 2 * out_shape.shape[0] * weight.size
    return call(finish_kernel, "finish", out_shape, (*parts, weight), flops, 2 * weight.size)


def tied(*values):
    return lax.optimization_barrier(values)


def shards(target, query_weight, source_keys, source_values, out_weight):
    groups = lax.axis_size("head")
    rows, depth = target.shape
    keys = (source_keys, move(source_keys, dcore=1))
    other_values = move(source_values, dcore=1)
    gathered = exchange(repeat(target, groups))
    queries = project(gathered.reshape(groups * rows, depth), query_weight)
    few = queries.shape[0]
    queries, source_values = tied(queries, source_values)
    partner, turned = tied(move(queries, dx=1), turn(source_values))
    mine = jnp.concatenate([queries, partner], axis=0)
    sibling, other_values = tied(move(mine, dcore=1), other_values)
    near = carry(jnp.concatenate([mine, sibling], axis=0), 1)
    values = (turned, turn(other_values))
    part_own, = attend((mine,), keys, values)
    part_own, near = tied(part_own, near)
    second = carry(near, 1)
    part, = attend((near,), keys, values)
    part, second = tied(part, second)
    third, far = carry(second, 1), carry(second[: 2 * few], 2)
    back_near = carry(part, -1)
    part_others, = attend((second[2 * few :],), keys, values)
    part_others, third, back_near = tied(part_others, third, back_near)
    back_others = carry(part_others, -2)
    part, = attend((third,), keys, values)
    part, second, far, back_others = tied(part, second, far, back_others)
    back_third = carry(part, -3)
    part_far, = attend((far,), keys, values)
    part_far, second = tied(part_far, second)
    back_far = carry(part_far, -4)
    part, = attend((second[: 2 * few],), keys, values)
    early = merge(2 * few, (part_own, 0), (back_far, 0), (back_near, 0), (back_third, 0), flops=MERGE_FLOPS)
    others = move(merge(2 * few, (back_others, 0), (back_near, 2 * few), (back_third, 2 * few)), dcore=1)
    back_second, early, others = tied(carry(part, -2), early, others)
    kept = merge(2 * few, (early, 0), (back_second, 0))
    other = move(merge(few, (kept, few), (others, few)), dx=1)
    projected = finish((kept, others, other), out_weight)
    received = exchange(projected.reshape(groups, rows, depth))
    return jnp.sum(received.astype(jnp.float32), axis=0).astype(jnp.bfloat16)


def solution(mesh):
    in_specs = (
        P(("ctx", "head"), None),
        P(None, "head"),
        P("ctx", "head"),
        P("ctx", "head"),
        P("head", None),
    )
    out_specs = P(("ctx", "head"), None)
    return jax.shard_map(shards, mesh=mesh, in_specs=in_specs, out_specs=out_specs, check_vma=False)
```

```python
import functools
import math

import jax
import jax.numpy as jnp
from jax import lax
from jax.experimental import pallas as pl
from jax.experimental.pallas import tpu as pltpu
from jax.sharding import PartitionSpec as P

HD = 128
BLOCK = 512
GROUP = 1024
PART = 64
TAIL = 16
AHEAD = 2
MERGE_FLOPS = 10**10
LOG2E = math.log2(math.e)
Z = 8


def vmem():
    return pl.BlockSpec(memory_space=pltpu.VMEM)


def move(value, dz=0, dx=0, dcore=0):
    pairs = []
    for source in range(Z * 4):
        z, x, core = source // 4, source // 2 % 2, source % 2
        pairs.append((source, (z + dz) % Z * 4 + (x ^ dx) * 2 + (core ^ dcore)))
    return lax.ppermute(value, "ctx", pairs)


def carry(value, steps):
    pairs = []
    for source in range(Z * 4):
        z, core = source // 4, source % 2
        pairs.append((source, (z + (-steps if core else steps)) % Z * 4 + source % 4))
    return lax.ppermute(value, "ctx", pairs)


def exchange(value):
    return lax.all_to_all(value, "head", 0, 0)


def parts_of(level):
    high = level.astype(jnp.bfloat16).astype(jnp.float32)
    middle = (level - high).astype(jnp.bfloat16).astype(jnp.float32)
    return high, middle, level - high - middle


def project_kernel(rows, weight, out):
    result = jnp.dot(rows[...], weight[...], preferred_element_type=jnp.float32)
    out[...] = (result * (1.0 / math.sqrt(HD))).astype(jnp.bfloat16)


def repeat_kernel(value, out):
    for at in range(out.shape[0]):
        out[at] = value[...]


def attend_kernel(count, *refs):
    asked, (key_a, key_b, value_a, value_b), rest = refs[:count], refs[count : count + 4], refs[count + 4 :]
    outs, held, weights = rest[:count], rest[count : count + AHEAD + 1], rest[count + AHEAD + 1 :]
    heads = asked[0].shape[1] // HD
    half = key_a.shape[0]
    across = sum(ref.shape[0] for ref in asked)
    steps = [(head, at) for head in range(heads) for at in range(0, 2 * half, GROUP)]
    row = lax.broadcasted_iota(jnp.int32, (TAIL, across), 0)

    def columns(head):
        return slice(head * HD, (head + 1) * HD)

    def turned_queries(head):
        return jnp.transpose(jnp.concatenate([ref[:, columns(head)] for ref in asked], axis=0))

    queries = [turned_queries(head) for head in range(heads)]

    def score(step, part, peak):
        head, at = steps[step]
        keys, place = (key_a, at + part) if at < half else (key_b, at + part - half)
        block = jnp.dot(
            keys[place : place + BLOCK, columns(head)], queries[head], preferred_element_type=jnp.float32
        )
        held[step % len(held)][part : part + BLOCK, :] = block
        top = jnp.max(block.reshape(BLOCK // 8, 8, across), axis=0)
        return top if peak is None else jnp.maximum(peak, top)

    def weigh(step, start, peak, total):
        for part in range(start, start + BLOCK, PART):
            block = held[step % len(held)][part : part + PART, :].reshape(PART // 8, 8, across)
            block = jnp.exp2(LOG2E * block - peak[None])
            total = total + jnp.sum(block, axis=0)
            block = block.reshape(PART, across).astype(jnp.bfloat16)
            weights[step % 2][part : part + PART, :] = block
        return total

    def weighted(step):
        head, at = steps[step]
        values, place = (value_a, at) if at < half else (value_b, at - half)
        return jnp.dot(
            values[columns(head), place : place + GROUP],
            weights[step % 2][...],
            preferred_element_type=jnp.float32,
        )

    stats = jnp.zeros((TAIL, across), jnp.float32)
    numerator = None

    def add_values(step, rescale, top, total):
        nonlocal numerator, stats
        head, at = steps[step]
        here = weighted(step)
        numerator = here if at == 0 else numerator * rescale + here
        if at + GROUP == 2 * half:
            total = jnp.sum(total, axis=0, keepdims=True)
            partial = jnp.transpose(numerator / total).astype(jnp.bfloat16)
            place = 0
            for ref, out in zip(asked, outs):
                out[: ref.shape[0], columns(head)] = partial[place : place + ref.shape[0]]
                place += ref.shape[0]
            for index, part in enumerate(parts_of(top + LOG2E * jnp.log(total))):
                stats = jnp.where(row == head * 3 + index, part, stats)

    peaks = [None] * len(steps)

    def score_ahead(step, part):
        if step < len(steps):
            peaks[step] = score(step, part, peaks[step])

    for step in range(AHEAD):
        for part in range(0, GROUP, BLOCK):
            score_ahead(step, part)
    pending = top = total = None
    for step, (head, at) in enumerate(steps):
        rescale, highest = None, LOG2E * jnp.max(peaks[step], axis=0, keepdims=True)
        if at:
            highest = jnp.maximum(top, highest)
            rescale = jnp.exp2(top - highest)
            total = total * rescale
        else:
            total = jnp.zeros((8, across), jnp.float32)
        top = highest
        wide = jnp.broadcast_to(top, (8, across))
        for part in range(0, GROUP, BLOCK):
            score_ahead(step + AHEAD, part)
            total = weigh(step, part, wide, total)
            if part == 0 and pending:
                add_values(*pending)
        pending = (step, rescale, top, total)
    add_values(*pending)
    stats = stats.astype(jnp.bfloat16)
    place = 0
    for ref, out in zip(asked, outs):
        rows = ref.shape[0]
        out[rows:, :] = jnp.zeros((TAIL, heads * HD), jnp.bfloat16)
        out[rows:, :rows] = stats[:, place : place + rows]
        place += rows


def merged(parts, tails):
    rows = parts[0].shape[0]
    heads = parts[0].shape[1] // HD
    shares, levels = [], []
    for head in range(heads):
        heights = [sum(tail[3 * head + index : 3 * head + index + 1, :] for index in range(3)) for tail in tails]
        peak = heights[0]
        for height in heights[1:]:
            peak = jnp.maximum(peak, height)
        powers = [jnp.exp2(height - peak) for height in heights]
        total = sum(powers)
        shares += [power / total for power in powers]
        levels.append(peak + LOG2E * jnp.log(total))
    place = lax.broadcasted_iota(jnp.int32, (HD, rows), 0)
    table = jnp.zeros((HD, rows), jnp.float32)
    for index, share in enumerate(shares):
        table = jnp.where(place == index, share, table)
    table = jnp.transpose(table)
    means = []
    for head in range(heads):
        columns = slice(head * HD, (head + 1) * HD)
        mean = 0.0
        for index, part in enumerate(parts):
            at = head * len(parts) + index
            mean += table[:, at : at + 1] * part[:, columns].astype(jnp.float32)
        means.append(mean.astype(jnp.bfloat16))
    return jnp.concatenate(means, axis=1), levels


def tail_of(levels):
    width = levels[0].shape[1]
    row = lax.broadcasted_iota(jnp.int32, (TAIL, width), 0)
    tail = jnp.zeros((TAIL, width), jnp.float32)
    for head, level in enumerate(levels):
        for index, part in enumerate(parts_of(level)):
            tail = jnp.where(row == head * 3 + index, part, tail)
    return tail.astype(jnp.bfloat16)


def piece(ref, start, rows):
    tail = ref[ref.shape[0] - TAIL :, start : start + rows].astype(jnp.float32)
    return ref[start : start + rows, :], tail


def merge_kernel(starts, *refs):
    out = refs[-1]
    rows = out.shape[0] - TAIL
    mean, levels = merged(*zip(*[piece(ref, start, rows) for ref, start in zip(refs, starts)]))
    out[:rows, :] = mean
    out[rows:, :] = jnp.zeros((TAIL, out.shape[1]), jnp.bfloat16)
    out[rows:, :rows] = tail_of(levels)


def finish_kernel(*refs):
    weight, out = refs[-2:]
    rows = out.shape[0]
    mixed, _ = merged(*zip(*[piece(ref, 0, rows) for ref in refs[:-2]]))
    out[...] = jnp.dot(mixed, weight[...], preferred_element_type=jnp.float32).astype(jnp.bfloat16)


def call(kernel, name, out_shape, operands, flops=0, read=0, exps=0, limit=16, scratch=()):
    return pl.pallas_call(
        kernel,
        out_shape=out_shape,
        in_specs=[vmem()] * len(operands),
        out_specs=jax.tree.map(lambda _: vmem(), out_shape),
        scratch_shapes=scratch,
        compiler_params=pltpu.CompilerParams(vmem_limit_bytes=limit << 20),
        cost_estimate=pl.CostEstimate(flops=flops, bytes_accessed=read, transcendentals=exps),
        name=name,
    )(*operands)


def shape(*dims):
    return jax.ShapeDtypeStruct(dims, jnp.bfloat16)


def project(rows, weight):
    out_shape = shape(rows.shape[0], weight.shape[1])
    flops = 2 * rows.shape[0] * weight.size
    return call(project_kernel, "project", out_shape, (rows, weight), flops, 2 * weight.size)


def repeat(value, count):
    return call(repeat_kernel, "repeat", shape(count, *value.shape), (value,), MERGE_FLOPS)


def attend(asked, keys, values):
    width = asked[0].shape[1]
    across = sum(queries.shape[0] for queries in asked)
    pairs = 2 * across * keys[0].shape[0] * (width // HD)
    out_shape = [shape(queries.shape[0] + TAIL, width) for queries in asked]
    scratch = [pltpu.VMEM((GROUP, across), kind) for kind in (jnp.float32,) * (AHEAD + 1) + (jnp.bfloat16,) * 2]
    kernel = functools.partial(attend_kernel, len(asked))
    operands = (*asked, *keys, *values)
    return call(kernel, "attend", out_shape, operands, 8 * pairs * HD, 8 * keys[0].size, pairs, 32, scratch)


def turn_kernel(value, out):
    for head in range(value.shape[1] // HD):
        out[head * HD : (head + 1) * HD, :] = jnp.transpose(value[:, head * HD : (head + 1) * HD])


def turn(value):
    return call(turn_kernel, "turn", shape(*value.shape[::-1]), (value,), 0, 4 * value.size)


def merge(rows, *places, flops=0):
    parts, starts = zip(*places)
    out_shape = shape(rows + TAIL, parts[0].shape[1])
    return call(functools.partial(merge_kernel, starts), "merge", out_shape, parts, flops)


def finish(parts, weight):
    out_shape = shape(parts[-1].shape[0] - TAIL, weight.shape[1])
    flops = 2 * out_shape.shape[0] * weight.size
    return call(finish_kernel, "finish", out_shape, (*parts, weight), flops, 2 * weight.size)


def tied(*values):
    return lax.optimization_barrier(values)


def shards(target, query_weight, source_keys, source_values, out_weight):
    groups = lax.axis_size("head")
    rows, depth = target.shape
    keys = (source_keys, move(source_keys, dcore=1))
    other_values = move(source_values, dcore=1)
    gathered = exchange(repeat(target, groups))
    queries = project(gathered.reshape(groups * rows, depth), query_weight)
    few = queries.shape[0]
    queries, source_values = tied(queries, source_values)
    partner, turned = tied(move(queries, dx=1), turn(source_values))
    mine = jnp.concatenate([queries, partner], axis=0)
    sibling, other_values = tied(move(mine, dcore=1), other_values)
    near = carry(jnp.concatenate([mine, sibling], axis=0), 1)
    values = (turned, turn(other_values))
    part_own, = attend((mine,), keys, values)
    part_own, near = tied(part_own, near)
    second = carry(near, 1)
    part, = attend((near,), keys, values)
    part, second = tied(part, second)
    third, far = carry(second, 1), carry(second[: 2 * few], 2)
    back_near = carry(part, -1)
    part_others, = attend((second[2 * few :],), keys, values)
    part_others, far, back_near = tied(part_others, far, back_near)
    back_others = carry(part_others, -2)
    part_far, = attend((far,), keys, values)
    part_far, third = tied(part_far, third)
    back_far = carry(part_far, -4)
    part, = attend((third,), keys, values)
    part, second, back_others = tied(part, second, back_others)
    back_third = carry(part, -3)
    part, = attend((second[: 2 * few],), keys, values)
    early = merge(2 * few, (part_own, 0), (back_far, 0), (back_near, 0), (back_third, 0), flops=MERGE_FLOPS)
    others = move(merge(2 * few, (back_others, 0), (back_near, 2 * few), (back_third, 2 * few)), dcore=1)
    back_second, early, others = tied(carry(part, -2), early, others)
    kept = merge(2 * few, (early, 0), (back_second, 0))
    other = move(merge(few, (kept, few), (others, few)), dx=1)
    projected = finish((kept, others, other), out_weight)
    received = exchange(projected.reshape(groups, rows, depth))
    return jnp.sum(received.astype(jnp.float32), axis=0).astype(jnp.bfloat16)


def solution(mesh):
    in_specs = (
        P(("ctx", "head"), None),
        P(None, "head"),
        P("ctx", "head"),
        P("ctx", "head"),
        P("head", None),
    )
    out_specs = P(("ctx", "head"), None)
    return jax.shard_map(shards, mesh=mesh, in_specs=in_specs, out_specs=out_specs, check_vma=False)
```

```python
import functools
import math

import jax
import jax.numpy as jnp
from jax import lax
from jax.experimental import pallas as pl
from jax.experimental.pallas import tpu as pltpu
from jax.sharding import PartitionSpec as P

HD = 128
BLOCK = 512
GROUP = 1024
PART = 64
TAIL = 16
AHEAD = 2
MERGE_FLOPS = 10**10
LOG2E = math.log2(math.e)
Z = 8


def vmem():
    return pl.BlockSpec(memory_space=pltpu.VMEM)


def move(value, dz=0, dx=0, dcore=0):
    pairs = []
    for source in range(Z * 4):
        z, x, core = source // 4, source // 2 % 2, source % 2
        pairs.append((source, (z + dz) % Z * 4 + (x ^ dx) * 2 + (core ^ dcore)))
    return lax.ppermute(value, "ctx", pairs)


def carry(value, steps):
    pairs = []
    for source in range(Z * 4):
        z, core = source // 4, source % 2
        pairs.append((source, (z + (-steps if core else steps)) % Z * 4 + source % 4))
    return lax.ppermute(value, "ctx", pairs)


def exchange(value):
    return lax.all_to_all(value, "head", 0, 0)


def parts_of(level):
    high = level.astype(jnp.bfloat16).astype(jnp.float32)
    middle = (level - high).astype(jnp.bfloat16).astype(jnp.float32)
    return high, middle, level - high - middle


def project_kernel(rows, weight, out):
    result = jnp.dot(rows[...], weight[...], preferred_element_type=jnp.float32)
    out[...] = (result * (1.0 / math.sqrt(HD))).astype(jnp.bfloat16)


def repeat_kernel(value, out):
    for at in range(out.shape[0]):
        out[at] = value[...]


def attend_kernel(count, *refs):
    asked, (key_a, key_b, value_a, value_b), rest = refs[:count], refs[count : count + 4], refs[count + 4 :]
    outs, held, weights = rest[:count], rest[count : count + AHEAD + 1], rest[count + AHEAD + 1 :]
    heads = asked[0].shape[1] // HD
    half = key_a.shape[0]
    across = sum(ref.shape[0] for ref in asked)
    steps = [(head, at) for head in range(heads) for at in range(0, 2 * half, GROUP)]
    row = lax.broadcasted_iota(jnp.int32, (TAIL, across), 0)

    def columns(head):
        return slice(head * HD, (head + 1) * HD)

    def turned_queries(head):
        return jnp.transpose(jnp.concatenate([ref[:, columns(head)] for ref in asked], axis=0))

    queries = [turned_queries(head) for head in range(heads)]

    def score(step, part, peak):
        head, at = steps[step]
        keys, place = (key_a, at + part) if at < half else (key_b, at + part - half)
        block = jnp.dot(
            keys[place : place + BLOCK, columns(head)], queries[head], preferred_element_type=jnp.float32
        )
        held[step % len(held)][part : part + BLOCK, :] = block
        top = jnp.max(block.reshape(BLOCK // 8, 8, across), axis=0)
        return top if peak is None else jnp.maximum(peak, top)

    def weigh(step, start, peak, total):
        for part in range(start, start + BLOCK, PART):
            block = held[step % len(held)][part : part + PART, :].reshape(PART // 8, 8, across)
            block = jnp.exp2(LOG2E * block - peak[None])
            total = total + jnp.sum(block, axis=0)
            block = block.reshape(PART, across).astype(jnp.bfloat16)
            weights[step % 2][part : part + PART, :] = block
        return total

    def weighted(step):
        head, at = steps[step]
        values, place = (value_a, at) if at < half else (value_b, at - half)
        return jnp.dot(
            values[columns(head), place : place + GROUP],
            weights[step % 2][...],
            preferred_element_type=jnp.float32,
        )

    stats = jnp.zeros((TAIL, across), jnp.float32)
    numerator = None

    def add_values(step, rescale, top, total):
        nonlocal numerator, stats
        head, at = steps[step]
        here = weighted(step)
        numerator = here if at == 0 else numerator * rescale + here
        if at + GROUP == 2 * half:
            total = jnp.sum(total, axis=0, keepdims=True)
            partial = jnp.transpose(numerator / total).astype(jnp.bfloat16)
            place = 0
            for ref, out in zip(asked, outs):
                out[: ref.shape[0], columns(head)] = partial[place : place + ref.shape[0]]
                place += ref.shape[0]
            for index, part in enumerate(parts_of(top + LOG2E * jnp.log(total))):
                stats = jnp.where(row == head * 3 + index, part, stats)

    peaks = [None] * len(steps)

    def score_ahead(step, part):
        if step < len(steps):
            peaks[step] = score(step, part, peaks[step])

    for step in range(AHEAD):
        for part in range(0, GROUP, BLOCK):
            score_ahead(step, part)
    pending = top = total = None
    for step, (head, at) in enumerate(steps):
        rescale, highest = None, LOG2E * jnp.max(peaks[step], axis=0, keepdims=True)
        if at:
            highest = jnp.maximum(top, highest)
            rescale = jnp.exp2(top - highest)
            total = total * rescale
        else:
            total = jnp.zeros((8, across), jnp.float32)
        top = highest
        wide = jnp.broadcast_to(top, (8, across))
        for part in range(0, GROUP, BLOCK):
            score_ahead(step + AHEAD, part)
            total = weigh(step, part, wide, total)
            if part == 0 and pending:
                add_values(*pending)
        pending = (step, rescale, top, total)
    add_values(*pending)
    stats = stats.astype(jnp.bfloat16)
    place = 0
    for ref, out in zip(asked, outs):
        rows = ref.shape[0]
        out[rows:, :] = jnp.zeros((TAIL, heads * HD), jnp.bfloat16)
        out[rows:, :rows] = stats[:, place : place + rows]
        place += rows


def merged(parts, tails):
    rows = parts[0].shape[0]
    heads = parts[0].shape[1] // HD
    shares, levels = [], []
    for head in range(heads):
        heights = [sum(tail[3 * head + index : 3 * head + index + 1, :] for index in range(3)) for tail in tails]
        peak = heights[0]
        for height in heights[1:]:
            peak = jnp.maximum(peak, height)
        powers = [jnp.exp2(height - peak) for height in heights]
        total = sum(powers)
        shares += [power / total for power in powers]
        levels.append(peak + LOG2E * jnp.log(total))
    place = lax.broadcasted_iota(jnp.int32, (HD, rows), 0)
    table = jnp.zeros((HD, rows), jnp.float32)
    for index, share in enumerate(shares):
        table = jnp.where(place == index, share, table)
    table = jnp.transpose(table)
    means = []
    for head in range(heads):
        columns = slice(head * HD, (head + 1) * HD)
        mean = 0.0
        for index, part in enumerate(parts):
            at = head * len(parts) + index
            mean += table[:, at : at + 1] * part[:, columns].astype(jnp.float32)
        means.append(mean.astype(jnp.bfloat16))
    return jnp.concatenate(means, axis=1), levels


def tail_of(levels):
    width = levels[0].shape[1]
    row = lax.broadcasted_iota(jnp.int32, (TAIL, width), 0)
    tail = jnp.zeros((TAIL, width), jnp.float32)
    for head, level in enumerate(levels):
        for index, part in enumerate(parts_of(level)):
            tail = jnp.where(row == head * 3 + index, part, tail)
    return tail.astype(jnp.bfloat16)


def piece(ref, start, rows):
    tail = ref[ref.shape[0] - TAIL :, start : start + rows].astype(jnp.float32)
    return ref[start : start + rows, :], tail


def merge_kernel(starts, *refs):
    out = refs[-1]
    rows = out.shape[0] - TAIL
    mean, levels = merged(*zip(*[piece(ref, start, rows) for ref, start in zip(refs, starts)]))
    out[:rows, :] = mean
    out[rows:, :] = jnp.zeros((TAIL, out.shape[1]), jnp.bfloat16)
    out[rows:, :rows] = tail_of(levels)


def finish_kernel(*refs):
    weight, out = refs[-2:]
    rows = out.shape[0]
    mixed, _ = merged(*zip(*[piece(ref, 0, rows) for ref in refs[:-2]]))
    out[...] = jnp.dot(mixed, weight[...], preferred_element_type=jnp.float32).astype(jnp.bfloat16)


def call(kernel, name, out_shape, operands, flops=0, read=0, exps=0, limit=16, scratch=()):
    return pl.pallas_call(
        kernel,
        out_shape=out_shape,
        in_specs=[vmem()] * len(operands),
        out_specs=jax.tree.map(lambda _: vmem(), out_shape),
        scratch_shapes=scratch,
        compiler_params=pltpu.CompilerParams(vmem_limit_bytes=limit << 20),
        cost_estimate=pl.CostEstimate(flops=flops, bytes_accessed=read, transcendentals=exps),
        name=name,
    )(*operands)


def shape(*dims):
    return jax.ShapeDtypeStruct(dims, jnp.bfloat16)


def project(rows, weight):
    out_shape = shape(rows.shape[0], weight.shape[1])
    flops = 2 * rows.shape[0] * weight.size
    return call(project_kernel, "project", out_shape, (rows, weight), flops, 2 * weight.size)


def repeat(value, count):
    return call(repeat_kernel, "repeat", shape(count, *value.shape), (value,), MERGE_FLOPS)


def attend(asked, keys, values):
    width = asked[0].shape[1]
    across = sum(queries.shape[0] for queries in asked)
    pairs = 2 * across * keys[0].shape[0] * (width // HD)
    out_shape = [shape(queries.shape[0] + TAIL, width) for queries in asked]
    scratch = [pltpu.VMEM((GROUP, across), kind) for kind in (jnp.float32,) * (AHEAD + 1) + (jnp.bfloat16,) * 2]
    kernel = functools.partial(attend_kernel, len(asked))
    operands = (*asked, *keys, *values)
    return call(kernel, "attend", out_shape, operands, 8 * pairs * HD, 8 * keys[0].size, pairs, 32, scratch)


def turn_kernel(value, out):
    for head in range(value.shape[1] // HD):
        out[head * HD : (head + 1) * HD, :] = jnp.transpose(value[:, head * HD : (head + 1) * HD])


def turn(value):
    return call(turn_kernel, "turn", shape(*value.shape[::-1]), (value,), 0, 4 * value.size)


def merge(rows, *places, flops=0):
    parts, starts = zip(*places)
    out_shape = shape(rows + TAIL, parts[0].shape[1])
    return call(functools.partial(merge_kernel, starts), "merge", out_shape, parts, flops)


def finish(parts, weight):
    out_shape = shape(parts[-1].shape[0] - TAIL, weight.shape[1])
    flops = 2 * out_shape.shape[0] * weight.size
    return call(finish_kernel, "finish", out_shape, (*parts, weight), flops, 2 * weight.size)


def tied(*values):
    return lax.optimization_barrier(values)


def shards(target, query_weight, source_keys, source_values, out_weight):
    groups = lax.axis_size("head")
    rows, depth = target.shape
    keys = (source_keys, move(source_keys, dcore=1))
    other_values = move(source_values, dcore=1)
    gathered = exchange(repeat(target, groups))
    queries = project(gathered.reshape(groups * rows, depth), query_weight)
    few = queries.shape[0]
    queries, source_values = tied(queries, source_values)
    partner, turned = tied(move(queries, dx=1), turn(source_values))
    mine = jnp.concatenate([queries, partner], axis=0)
    sibling, other_values = tied(move(mine, dcore=1), other_values)
    near = carry(jnp.concatenate([mine, sibling], axis=0), 1)
    values = (turned, turn(other_values))
    part_own, = attend((mine,), keys, values)
    part_own, near = tied(part_own, near)
    second = carry(near, 1)
    part, = attend((near,), keys, values)
    part, second = tied(part, second)
    third, far = carry(second, 1), carry(second[: 2 * few], 2)
    back_near = carry(part, -1)
    part_others, = attend((second[2 * few :],), keys, values)
    part_others, third, back_near = tied(part_others, third, back_near)
    back_others = carry(part_others, -2)
    part, = attend((third,), keys, values)
    part, second, far = tied(part, second, far)
    back_third = carry(part, -3)
    part_far, = attend((far,), keys, values)
    part_far, second = tied(part_far, second)
    back_far = carry(part_far, -4)
    part, = attend((second[: 2 * few],), keys, values)
    part, back_others = tied(part, back_others)
    early = merge(2 * few, (part_own, 0), (back_far, 0), (back_near, 0), (back_third, 0), flops=MERGE_FLOPS)
    others = move(merge(2 * few, (back_others, 0), (back_near, 2 * few), (back_third, 2 * few)), dcore=1)
    back_second, early, others = tied(carry(part, -2), early, others)
    kept = merge(2 * few, (early, 0), (back_second, 0))
    other = move(merge(few, (kept, few), (others, few)), dx=1)
    projected = finish((kept, others, other), out_weight)
    received = exchange(projected.reshape(groups, rows, depth))
    return jnp.sum(received.astype(jnp.float32), axis=0).astype(jnp.bfloat16)


def solution(mesh):
    in_specs = (
        P(("ctx", "head"), None),
        P(None, "head"),
        P("ctx", "head"),
        P("ctx", "head"),
        P("head", None),
    )
    out_specs = P(("ctx", "head"), None)
    return jax.shard_map(shards, mesh=mesh, in_specs=in_specs, out_specs=out_specs, check_vma=False)
```
